256 devices in a mesh: seq: 32 (over x, y, core), kv: 8 (over z).
Axes of the slice: x: 4, y: 4, z: 8, core: 2. Of those that a mesh axis runs over, the one named last changes fastest.
Arguments:
- query_rows: bfloat16 [8192, 8192], P(('seq', 'kv')), may hold values from -6 to 6
- attn_out: bfloat16 [8192, 8192], P(('seq', 'kv')), may hold values from -3 to 3
- grad_out: bfloat16 [8192, 8192], P(('seq', 'kv')), may hold values from -48 to 48
- logsumexp: float32 [64, 8192], P('kv', 'seq'), may hold values from 2.5 to 10.5
- key_cache: bfloat16 [8, 16384, 128], P('kv', 'seq'), may hold values from -6 to 6
- value_cache: bfloat16 [8, 16384, 128], P('kv', 'seq'), may hold values from -6 to 6
- block_lists: int32 [64, 64, 32], P('kv', 'seq'), may hold values from 0 to 127, as said below
- block_counts: int32 [64, 64], P('kv', 'seq'), may hold values from 2 to 32
Outputs:
- grad_query: bfloat16 [8192, 8192], P(('seq', 'kv'))
- grad_key: bfloat16 [8, 16384, 128], P('kv', 'seq')
- grad_value: bfloat16 [8, 16384, 128], P('kv', 'seq')
The draws below stay inside these ranges and needn't reach their ends.
Inputs may be any that keep to these rules, and one draw needn't show every extreme that they name: `block_lists`: for head h and query block q (context block 64 + q), entries 0 to block_counts[h, q] - 1 are distinct KV blocks, none after the query block's own block, entry 0 being that own block; later entries are 0. Over the heads of one KV group and the query blocks of one seq index, the lists name at most 2 distinct blocks among the 4 blocks of any one seq index, and in every draw there is a seq index whose blocks are named exactly 2 distinct times by every group at every seq index.
All inputs are finite; a program needn't handle non-finite values.
Results may differ from the reference program's by a relative error of at most 0.018.
Values may be sent and summed in bfloat16 or wider, within the bound.
A program may use at most 64 MiB of HBM per device.

```python
import math
import jax
import jax.numpy as jnp
from jax import lax

HEADS = 64
KVG = 8
HD = 128
BLK = 128
NQB = 2
KVB = 4
QN = 8192
CTX = 16384
QB = 64
NB = 128
SMAX = 32


def selection_plan(key):
    seq_count = QB // NQB
    per_group = HEADS // KVG
    count_table = jnp.array([2, 2, 3, 4, 4, 5, 6, 6, 8, 8, 10, 12, 16, 32], jnp.int32)
    picked = jax.random.randint(jax.random.fold_in(key, 101), (HEADS, QB), 0, 14)
    counts = jnp.minimum(count_table[picked], SMAX)
    counts = counts.at[0, 0].set(SMAX).at[1, 0].set(2)
    block_ids = jnp.arange(NB, dtype=jnp.int32)
    first_blocks = QB + jnp.arange(seq_count, dtype=jnp.int32) * NQB
    own_zone = (block_ids[None, :] >= first_blocks[:, None]) & (block_ids[None, :] < first_blocks[:, None] + NQB)
    earlier = block_ids[None, :] < first_blocks[:, None]
    noise_draw = jax.random.randint(jax.random.fold_in(key, 102), (KVG, seq_count, NB), 0, 65536) * NB + block_ids
    ranking = jnp.where(own_zone[None], block_ids - NB, jnp.where(earlier[None], noise_draw, 1073741824 + block_ids))
    grouped = ranking.reshape(KVG, seq_count, NB // KVB, KVB)
    owner_rank = jnp.sum(grouped[..., None, :] < grouped[..., :, None], axis=-1)
    allowed = ((owner_rank < NQB) & (grouped < 1073741824)).reshape(KVG, seq_count, NB)
    owner_rank = owner_rank.reshape(KVG, seq_count, NB)
    forced_owner = jax.random.randint(jax.random.fold_in(key, 103), (), 0, seq_count // 2)
    owner_cols = forced_owner * KVB + jnp.arange(KVB, dtype=jnp.int32)
    owner_allowed = jnp.take(allowed, owner_cols, axis=2)
    owner_ranks = jnp.take(owner_rank, owner_cols, axis=2)
    slot_ids = jnp.arange(NQB)
    forced_block = jnp.sum(jnp.where(owner_allowed[..., None] & (owner_ranks[..., None] == slot_ids), owner_cols[:, None], 0), axis=2)
    head_ids = jnp.arange(HEADS)[:, None]
    query_ids = jnp.arange(QB)[None, :]
    group_of = head_ids // per_group
    seq_of = query_ids // NQB
    slot_of = query_ids % NQB * per_group + head_ids % per_group
    forced = jnp.where(slot_of < NQB, forced_block[group_of, seq_of, jnp.minimum(slot_of, NQB - 1)], -1)
    row_allowed = allowed[group_of, seq_of]
    absolute = QB + jnp.arange(QB, dtype=jnp.int32)
    causal = block_ids[None, None, :] < absolute[None, :, None]
    own_hit = block_ids[None, None, :] == absolute[None, :, None]
    pinned = block_ids[None, None, :] == forced[..., None]
    row_noise = jax.random.randint(jax.random.fold_in(key, 104), (HEADS, QB, NB), 0, 65536) * NB + block_ids
    row_score = jnp.where(own_hit, -2, jnp.where(pinned, -1, jnp.where(row_allowed & causal, row_noise, 1073741824 + block_ids)))
    ordering = jnp.argsort(row_score, axis=-1)[..., :SMAX].astype(jnp.int32)
    live_slots = jnp.arange(SMAX) < counts[..., None]
    return (jnp.where(live_slots, ordering, 0).astype(jnp.int32), counts.astype(jnp.int32))


def draw_block_lists(key, part):
    return selection_plan(key)[0]


def draw_block_counts(key, part):
    return selection_plan(key)[1]


def draw_logsumexp(key, part):
    plan_counts = selection_plan(key)[1]
    key = jax.random.fold_in(key, 7)
    base_level = jnp.log(BLK * plan_counts.astype(jnp.float32)) + 0.5
    base_level = jnp.repeat(base_level, BLK, axis=1)
    jitter = jax.random.uniform(key, (HEADS, QN), jnp.float32, -0.5, 0.5)
    return base_level + jitter


def block_levels(rng, dims, shards, low, largest):
    loudness, own = 1.0, jax.random.fold_in(rng, 6)
    for dim, shards_of in shards:
        draws = jnp.exp(jax.random.uniform(jax.random.fold_in(own, dim), (shards_of,), jnp.float32, low / len(shards), largest / len(shards)))
        loudness = loudness * jnp.repeat(draws, dims[dim] // shards_of).reshape([-1 if axis == dim else 1 for axis in range(len(dims))])
    return loudness


def noise(key, shape, deviation, bound, pieces=(), held_as=jnp.bfloat16):
    gain = block_levels(key, shape, pieces, -0.22, 0.18) if pieces else 1.0
    entries = jax.random.normal(key, shape, jnp.float32) * deviation * gain
    return jnp.minimum(jnp.maximum(entries, -bound), bound).astype(held_as)


def setup_inputs(seed: int = 0) -> dict:
    key_list = jax.random.split(jax.random.key(seed), 9)
    return {
        "query_rows": noise(key_list[0], (QN, HEADS * HD), 1.0, 6.0, ((0, 256),)),
        "attn_out": noise(key_list[1], (QN, HEADS * HD), 0.5, 3.0, ((0, 256),)),
        "grad_out": noise(key_list[2], (QN, HEADS * HD), 8.0, 48.0, ((0, 256),)),
        "logsumexp": draw_logsumexp(jax.random.fold_in(key_list[8], 71), 0),
        "key_cache": noise(key_list[4], (KVG, CTX, HD), 1.0, 6.0, ((0, 8), (1, 32))),
        "value_cache": noise(key_list[5], (KVG, CTX, HD), 1.0, 6.0, ((0, 8), (1, 32))),
        "block_lists": draw_block_lists(jax.random.fold_in(key_list[8], 71), 0),
        "block_counts": draw_block_counts(jax.random.fold_in(key_list[8], 71), 0),
    }


def reference(query_rows, attn_out, grad_out, logsumexp, key_cache, value_cache, block_lists, block_counts):
    score_scale = 1.0 / math.sqrt(HD)
    per_group = HEADS // KVG
    seq_count = QB // NQB
    row_terms = lax.optimization_barrier(jnp.sum((grad_out.astype(jnp.float32) * attn_out.astype(jnp.float32)).reshape(QN, HEADS, HD), axis=2)).T
    query_heads = jnp.transpose(query_rows.reshape(seq_count, NQB, BLK, HEADS, HD), (0, 3, 1, 2, 4))
    grad_heads = jnp.transpose(grad_out.reshape(seq_count, NQB, BLK, HEADS, HD), (0, 3, 1, 2, 4))
    lse_heads = jnp.transpose(logsumexp.reshape(HEADS, seq_count, NQB, BLK), (1, 0, 2, 3))
    delta_heads = jnp.transpose(row_terms.reshape(HEADS, seq_count, NQB, BLK), (1, 0, 2, 3))
    list_heads = jnp.transpose(block_lists.reshape(HEADS, seq_count, NQB, SMAX), (1, 0, 2, 3))
    count_heads = jnp.transpose(block_counts.reshape(HEADS, seq_count, NQB), (1, 0, 2))
    paired = jnp.concatenate([key_cache, value_cache], axis=2).reshape(KVG, NB, BLK, 2 * HD)
    causal = jnp.arange(BLK)[None, :] <= jnp.arange(BLK)[:, None]
    positions = jnp.arange(SMAX).astype(jnp.int32)
    head_ids = jnp.arange(HEADS).astype(jnp.int32)

    def one_owner(total, owner_items):
        owner_id, query_p, grad_p, lse_p, delta_p, list_p, count_p = owner_items
        own_block = (QB + owner_id * NQB + jnp.arange(NQB)).astype(jnp.int32)

        def one_head(accum, items):
            head_id, query_h, grad_h, lse_h, delta_h, list_h, count_h = items
            group = head_id // per_group
            cache_h = lax.dynamic_index_in_dim(paired, group, 0, keepdims=False)
            tile_pairs = jnp.take(cache_h, list_h, axis=0).astype(jnp.float32)
            tile_keys = tile_pairs[..., :HD]
            tile_values = tile_pairs[..., HD:]
            query_f = query_h.astype(jnp.float32)
            grad_f = grad_h.astype(jnp.float32)
            scores = jnp.einsum('qtd,qjsd->qjts', query_f, tile_keys) * score_scale
            live_slots = positions[None, :] < count_h[:, None]
            diagonal = list_h == own_block[:, None]
            allowed = live_slots[..., None, None] & (jnp.logical_not(diagonal)[..., None, None] | causal)
            weights = jnp.where(allowed, jnp.exp(scores - lse_h[:, None, :, None]), 0.0)
            grad_weights = jnp.einsum('qtd,qjsd->qjts', grad_f, tile_values)
            grad_scores = weights * (grad_weights - delta_h[:, None, :, None])
            weights_half = lax.optimization_barrier(weights.astype(jnp.bfloat16)).astype(jnp.float32)
            scores_half = lax.optimization_barrier(grad_scores.astype(jnp.bfloat16)).astype(jnp.float32)
            query_grad = jnp.einsum('qjts,qjsd->qtd', scores_half, tile_keys) * score_scale
            key_terms = jnp.einsum('qjts,qtd->qjsd', scores_half, query_f)
            value_terms = jnp.einsum('qjts,qtd->qjsd', weights_half, grad_f)
            terms = jnp.concatenate([key_terms, value_terms], axis=3).reshape(NQB * SMAX, BLK, 2 * HD)
            accum = accum.at[group, list_h.reshape(-1)].add(terms)
            return (accum, query_grad.astype(jnp.bfloat16))
        fresh = jnp.zeros((KVG, NB, BLK, 2 * HD), jnp.float32)
        accum, query_grads = lax.scan(one_head, fresh, (head_ids, query_p, grad_p, lse_p, delta_p, list_p, count_p))
        partial_value = lax.optimization_barrier(accum.astype(jnp.bfloat16)).astype(jnp.float32)
        return (total + partial_value, query_grads)
    initial = jnp.zeros((KVG, NB, BLK, 2 * HD), jnp.float32)
    owner_ids = jnp.arange(seq_count).astype(jnp.int32)
    total, query_grads = lax.scan(one_owner, initial, (owner_ids, query_heads, grad_heads, lse_heads, delta_heads, list_heads, count_heads))
    grad_query = jnp.transpose(query_grads, (0, 2, 3, 1, 4)).reshape(QN, HEADS * HD)
    grad_key = (total[..., :HD] * score_scale).astype(jnp.bfloat16).reshape(KVG, CTX, HD)
    grad_value = total[..., HD:].astype(jnp.bfloat16).reshape(KVG, CTX, HD)
    return (grad_query, grad_key, grad_value)
```

```python
import math

import jax
import jax.numpy as jnp
from jax import lax
from jax.experimental import pallas as pl
from jax.experimental.pallas import tpu as pltpu
from jax.sharding import PartitionSpec as P

MESH = pl.DeviceIdType.MESH

G = 4
BLK = 128
LOG2E = math.log2(math.e)

def grads_kernel(lists, counts, q_ref, do_ref, lse_ref, dp_ref, k_ref, v_ref, dq_ref, dk_ref, dv_ref, acc, w1, w2, rowv, dqa):
    scale = 1.0 / math.sqrt(128.0)
    f32, bf = jnp.float32, jnp.bfloat16

    def zero(i, _):
        acc[i] = jnp.zeros((BLK, 256), f32)
        return 0
    lax.fori_loop(0, 128, zero, 0)
    w1[...] = jnp.zeros((256, 256), bf)
    w2[...] = jnp.zeros((256, 256), bf)
    for qb in range(2):
        d = dp_ref[4 * qb]
        for s in range(1, 4):
            d = d + pltpu.roll(dp_ref[4 * qb + s], 32 * s, 1)
        rowv[0, qb] = d
        rowv[1, qb] = lse_ref[:, qb * BLK:(qb + 1) * BLK] * LOG2E
    rows_i = lax.broadcasted_iota(jnp.int32, (BLK, BLK), 0)
    cols_i = lax.broadcasted_iota(jnp.int32, (BLK, BLK), 1)

    def one_row(r, _):
        h, qb = r // 2, lax.rem(r, 2)
        cs = pl.ds(pl.multiple_of(h * BLK, BLK), BLK)
        rs = pl.ds(pl.multiple_of(qb * BLK, BLK), BLK)
        q = q_ref[rs, cs]
        d = do_ref[rs, cs]
        w1[:BLK, :BLK] = q.T
        w1[BLK:, BLK:] = d.T
        w2[:BLK, :BLK] = q
        w2[BLK:, BLK:] = d
        dqa[...] = jnp.zeros((BLK, BLK), f32)
        delta = rowv[0, qb, pl.ds(h, 1), :]
        lse2 = rowv[1, qb, pl.ds(h, 1), :]
        count = counts[h, qb]

        def group(g, _):
            j0 = g * G
            bs = [lists[h, qb, j0 + i] for i in range(G)]
            ks = [k_ref[b] for b in bs]
            kv = jnp.concatenate([jnp.concatenate([ks[i], v_ref[bs[i]]], axis=1) for i in range(G)], axis=0)
            sd = jnp.dot(kv, w1[...], preferred_element_type=f32)
            dss, pds = [], []
            for i in range(G):
                s = sd[i * BLK:(i + 1) * BLK, :BLK]
                dpv = sd[i * BLK:(i + 1) * BLK, BLK:]
                bias = jnp.where(j0 + i < count, lse2, 1e30)
                p = jnp.exp2(s * (scale * LOG2E) - bias)
                if i == 0:
                    p = jnp.where((rows_i <= cols_i) | (g > 0), p, 0.0)
                ds = p * (dpv - delta)
                dsb = ds.astype(bf)
                dss.append(dsb)
                pds.append(jnp.concatenate([dsb, p.astype(bf)], axis=1))
            out = jnp.dot(jnp.concatenate(pds, axis=0), w2[...], preferred_element_type=f32)
            dst = jnp.concatenate([x.T for x in dss], axis=1)
            dqa[...] += jnp.dot(dst, jnp.concatenate(ks, axis=0), preferred_element_type=f32)
            for i in range(G):
                acc[bs[i]] += out[i * BLK:(i + 1) * BLK]
            return 0
        lax.fori_loop(0, (count + (G - 1)) // G, group, 0)
        dq_ref[rs, cs] = (dqa[...] * scale).astype(bf)
        return 0
    lax.fori_loop(0, 16, one_row, 0)

    def fin(i, _):
        a = acc[i]
        dk_ref[i] = a[:, :BLK].astype(bf)
        dv_ref[i] = a[:, BLK:].astype(bf)
        return 0
    lax.fori_loop(0, 128, fin, 0)

def grads(lists, counts, q, do, lse, dp, k, v):
    V = pl.BlockSpec(memory_space=pltpu.VMEM)
    S = pl.BlockSpec(memory_space=pltpu.SMEM)
    bf = jnp.bfloat16
    return pl.pallas_call(grads_kernel,
        out_shape=(jax.ShapeDtypeStruct((256, 1024), bf), jax.ShapeDtypeStruct((128, 128, 128), bf), jax.ShapeDtypeStruct((128, 128, 128), bf)),
        in_specs=[S, S] + [V] * 6, out_specs=(V, V, V),
        scratch_shapes=[pltpu.VMEM((128, 128, 256), jnp.float32), pltpu.VMEM((256, 256), bf), pltpu.VMEM((256, 256), bf), pltpu.VMEM((2, 2, 8, 128), jnp.float32), pltpu.VMEM((128, 128), jnp.float32)],
        compiler_params=pltpu.CompilerParams(vmem_limit_bytes=56 * 2**20))(lists, counts, q, do, lse, dp, k, v)


class Wires:
    def __init__(self, send_sem, recv_sem, local_sem):
        self.send_sem, self.recv_sem, self.local_sem = send_sem, recv_sem, local_sem
        self.count = 0
        self.local_count = 0
        self.started = []

    def send(self, src, dst, device):
        i = self.count
        self.count += 1
        copy = pltpu.make_async_remote_copy(
            src_ref=src,
            dst_ref=dst,
            send_sem=self.send_sem.at[i],
            recv_sem=self.recv_sem.at[i],
            device_id=device,
            device_id_type=MESH,
        )
        copy.start()
        self.started.append(copy)
        return copy

    def local(self, src, dst):
        i = self.local_count
        self.local_count += 1
        copy = pltpu.make_async_copy(src, dst, self.local_sem.at[i])
        copy.start()
        return copy

    def finish_sends(self):
        for copy in self.started:
            copy.wait_send()


def greet(devices):
    barrier = pltpu.get_barrier_semaphore()
    for device in devices:
        pl.semaphore_signal(barrier, inc=1, device_id=device, device_id_type=MESH)
    pl.semaphore_wait(barrier, len(devices))


def place():
    s = lax.axis_index("seq")
    x, y, c = s // 8, lax.rem(s // 2, 4), lax.rem(s, 2)

    def at(dx, dy, other=0):
        core = c if other == 0 else 1 - c
        return {"seq": (lax.rem(x + dx + 4, 4) * 4 + lax.rem(y + dy + 4, 4)) * 2 + core}

    return x, y, c, at


def wrap4(i):
    return lax.rem(i + 4, 4)


def spread_kernel(
    q_ref, o_ref, g_ref, k_ref, v_ref,
    qo_ref, go_ref, dp_ref, kf_ref, vf_ref,
    o_buf, g_buf, d_buf, send_sem, recv_sem, local_sem,
):
    me = lax.axis_index("kv")
    x, y, c, at = place()
    z_at = [{"kv": lax.rem(me + i, 8)} for i in range(8)]
    greet(z_at[1:] + [at(1, 0), at(-1, 0), at(0, 1), at(0, -1), at(0, 0, 1)])
    wires = Wires(send_sem, recv_sem, local_sem)
    locals_ = []
    waits = []

    load_o = wires.local(o_ref, o_buf)
    load_g = wires.local(g_ref, g_buf)

    class Ring:
        def __init__(self, src, full, x_first):
            self.src, self.full, self.x_first = src, full, x_first

        def dev(self, da, db):
            return at(da, db) if self.x_first else at(db, da)

        def slot(self, da, db, half=None):
            dx, dy = (da, db) if self.x_first else (db, da)
            ref = self.full.at[wrap4(x + dx), wrap4(y + dy), c]
            return ref if half is None else ref.at[pl.ds(half * 256, 256)]

        def put(self, ref, da, db):
            return wires.send(ref, ref, self.dev(da, db))

        def share(self, da, db):
            ref = self.slot(da, db)
            waits.append(wires.send(ref, ref, at(0, 0, 1)))

        def begin(self):
            own = self.slot(0, 0)
            self.ap = wires.send(self.src, own, self.dev(1, 0))
            self.am = wires.send(self.src, own, self.dev(-1, 0))
            self.bp = [wires.send(self.src, own, self.dev(0, 1))]
            self.bm = [wires.send(self.src, own, self.dev(0, -1))]

        def own(self):
            own = self.slot(0, 0)
            waits.append(wires.send(self.src, own, at(0, 0, 1)))
            locals_.append(wires.local(self.src, own))

        def both(self, ref):
            self.bp.append(self.put(ref, 0, 1))
            self.bm.append(self.put(ref, 0, -1))

        def first(self):
            self.ap.wait_recv()
            self.a2p = self.put(self.slot(-1, 0, 0), 1, 0)
            self.both(self.slot(-1, 0))
            self.am.wait_recv()
            self.a2m = self.put(self.slot(1, 0, 1), -1, 0)
            self.both(self.slot(1, 0))
            self.share(-1, 0)
            self.share(1, 0)

        def second(self):
            self.a2p.wait_recv()
            self.both(self.slot(2, 0, 0))
            self.a2m.wait_recv()
            self.both(self.slot(2, 0, 1))
            self.share(2, 0)

        def third(self, step):
            if step == 0:
                self.bp[0].wait_recv()
                self.c = [self.put(self.slot(0, -1), 0, 1)]
                self.share(0, -1)
                self.bm[0].wait_recv()
                self.share(0, 1)
            elif step == 1:
                self.bp[1].wait_recv()
                self.c.append(self.put(self.slot(-1, -1), 0, 1))
                self.share(-1, -1)
                self.bm[1].wait_recv()
                self.share(-1, 1)
            elif step == 2:
                self.bp[2].wait_recv()
                self.share(1, -1)
                self.bm[2].wait_recv()
                self.c.append(self.put(self.slot(1, 1), 0, -1))
                self.share(1, 1)
            else:
                self.bm[3].wait_recv()
                self.c.append(self.put(self.slot(2, 1, 0), 0, -1))
                self.bm[4].wait_recv()
                self.c.append(self.put(self.slot(2, 1, 1), 0, -1))
                self.share(2, 1)
                self.bp[3].wait_recv()
                self.bp[4].wait_recv()
                self.share(2, -1)

        def fourth(self, step):
            if step < 3:
                self.c[step].wait_recv()
                self.share((0, -1, 1)[step], 2)
            else:
                self.c[3].wait_recv()
                self.c[4].wait_recv()
                self.share(2, 2)

    rings = (Ring(k_ref, kf_ref, True), Ring(v_ref, vf_ref, False))
    for ring in rings:
        ring.begin()
    rows = pl.ds(pl.multiple_of(me * 32, 32), 32)

    def columns(i):
        return pl.ds(pl.multiple_of(lax.rem(me + i, 8) * 1024, 1024), 1024)

    for i in (4, 3, 5, 2, 6, 1, 7):
        for src, dst in ((q_ref, qo_ref), (g_ref, go_ref)):
            waits.append(wires.send(src.at[:, columns(i)], dst.at[rows, :], z_at[i]))
    for src, dst in ((q_ref, qo_ref), (g_ref, go_ref)):
        locals_.append(wires.local(src.at[:, columns(0)], dst.at[rows, :]))
    for ring in rings:
        ring.own()

    load_o.wait()
    load_g.wait()
    of_head = (
        lax.broadcasted_iota(jnp.int32, (8, 1024), 1) // 128
        == lax.broadcasted_iota(jnp.int32, (8, 1024), 0)
    ).astype(jnp.float32)
    d_buf[...] = jnp.zeros(d_buf.shape, jnp.float32)
    for group in range(8):
        cols = pl.ds(group * 1024, 1024)
        terms = o_buf[:, cols].astype(jnp.float32) * g_buf[:, cols].astype(jnp.float32)
        d_buf[group, :, :32] = lax.dot_general(
            of_head,
            terms,
            (((1,), (1,)), ((), ())),
            precision=lax.Precision.HIGHEST,
            preferred_element_type=jnp.float32,
        )
    for i in range(1, 8):
        waits.append(wires.send(d_buf.at[lax.rem(me + i, 8)], dp_ref.at[me], z_at[i]))
    locals_.append(wires.local(d_buf.at[me], dp_ref.at[me]))

    for ring in rings:
        ring.first()
    for ring in rings:
        ring.second()
    for step in range(4):
        for ring in rings:
            ring.third(step)
    for step in range(4):
        for ring in rings:
            ring.fourth(step)
    for copy in waits:
        copy.wait_recv()
    for copy in locals_:
        copy.wait()
    wires.finish_sends()


def collect_kernel(
    dq_ref, dk_ref, dv_ref,
    gq_ref, gk_ref, gv_ref,
    mine_k, mine_v, sib_k, sib_v, far_k, far_v, near_k, near_v, end_k, end_v,
    send_sem, recv_sem, local_sem,
):
    me = lax.axis_index("kv")
    x, y, c, at = place()
    z_at = [{"kv": lax.rem(me + i, 8)} for i in range(8)]
    greet(z_at[1:] + [at(1, 0), at(-1, 0), at(0, 1), at(0, -1), at(0, 0, 1)])
    wires = Wires(send_sem, recv_sem, local_sem)
    f32, bf16 = jnp.float32, jnp.bfloat16
    waits = []

    class Ring:
        def __init__(self, src, mine, sib, far, near, end, x_first):
            self.src, self.mine, self.sib = src, mine, sib
            self.far, self.near, self.end, self.x_first = far, near, end, x_first
            self.a, self.b = (x, y) if x_first else (y, x)

        def dev(self, da, db):
            return at(da, db) if self.x_first else at(db, da)

        def line(self, ref, db, core=None):
            b = wrap4(self.b + db)
            at_ = (slice(None), b) if self.x_first else (b, slice(None))
            return ref.at[at_] if core is None else ref.at[at_ + (core,)]

        def cell(self, ref, da, db):
            a, b = wrap4(self.a + da), wrap4(self.b + db)
            return ref.at[a, b] if self.x_first else ref.at[b, a]

        def begin(self, db):
            load = wires.local(self.line(self.src, db, c), self.line(self.mine, db))
            swap = wires.send(
                self.line(self.src, db, 1 - c), self.line(self.sib, db), at(0, 0, 1)
            )
            return load, swap

        def begin_all(self):
            self.swaps = {db: self.begin(db) for db in (2, 1, -1, 0)}

        def join(self, db):
            load, swap = self.swaps[db]
            load.wait()
            swap.wait_recv()
            for da in (2, 1, -1, 0):
                m = self.cell(self.mine, da, db)
                s = self.cell(self.sib, da, db)
                m[...] = (m[...].astype(f32) + s[...].astype(f32)).astype(bf16)

        def one(self):
            self.join(2)
            self.far_p = [
                wires.send(self.cell(self.mine, da, 2), self.far.at[0, i], self.dev(0, 1))
                for i, da in enumerate((2, 1))
            ]
            self.far_m = [
                wires.send(self.cell(self.mine, da, 2), self.far.at[1, i], self.dev(0, -1))
                for i, da in enumerate((-1, 0))
            ]

        def two(self):
            self.near_p, self.near_m = {}, {}
            self.join(1)
            for da in (-1, 0):
                self.near_p[da] = wires.send(
                    self.cell(self.mine, da, 1), self.near.at[0, da % 4], self.dev(0, 1)
                )
            self.join(-1)
            for da in (2, 1):
                self.near_m[da] = wires.send(
                    self.cell(self.mine, da, -1), self.near.at[1, da % 4], self.dev(0, -1)
                )

        def three(self, i):
            da = (2, 1)[i]
            self.far_p[i].wait_recv()
            m = self.cell(self.mine, da, 1)
            m[...] = (m[...].astype(f32) + self.far[0, i].astype(f32)).astype(bf16)
            self.near_p[da] = wires.send(m, self.near.at[0, da % 4], self.dev(0, 1))
            da = (-1, 0)[i]
            self.far_m[i].wait_recv()
            m = self.cell(self.mine, da, -1)
            m[...] = (m[...].astype(f32) + self.far[1, i].astype(f32)).astype(bf16)
            self.near_m[da] = wires.send(m, self.near.at[1, da % 4], self.dev(0, -1))

        def total(self, da):
            self.near_p[da].wait_recv()
            self.near_m[da].wait_recv()
            m = self.cell(self.mine, da, 0)
            return (
                m[...].astype(f32)
                + self.near[0, da % 4].astype(f32)
                + self.near[1, da % 4].astype(f32)
            )

        def four(self):
            m = self.cell(self.mine, 2, 0)
            m[...] = self.total(2).astype(bf16)
            lo, hi = pl.ds(0, 256), pl.ds(256, 256)
            self.end_far_p = wires.send(m.at[lo], self.end.at[0, lo], self.dev(1, 0))
            self.end_far_m = wires.send(m.at[hi], self.end.at[0, hi], self.dev(-1, 0))

        def five(self):
            lo, hi = pl.ds(0, 256), pl.ds(256, 256)
            mp = self.cell(self.mine, 1, 0)
            mm = self.cell(self.mine, -1, 0)
            tp = self.total(1)
            mp[...] = tp.astype(bf16)
            tm = self.total(-1)
            mm[...] = tm.astype(bf16)
            self.end_far_p.wait_recv()
            mp[:256] = (mp[:256].astype(f32) + self.end[0, :256].astype(f32)).astype(bf16)
            self.end_p = wires.send(mp, self.end.at[1], self.dev(1, 0))
            self.end_far_m.wait_recv()
            mm[256:] = (mm[256:].astype(f32) + self.end[0, 256:].astype(f32)).astype(bf16)
            self.end_m = wires.send(mm, self.end.at[2], self.dev(-1, 0))

        def six(self, out, scale):
            t = self.total(0)
            self.end_p.wait_recv()
            self.end_m.wait_recv()
            t = t + self.end[1].astype(f32) + self.end[2].astype(f32)
            out[...] = (t * scale).astype(bf16)

    rings = (
        Ring(dk_ref, mine_k, sib_k, far_k, near_k, end_k, True),
        Ring(dv_ref, mine_v, sib_v, far_v, near_v, end_v, False),
    )
    for db in (2, 1, -1, 0):
        for ring in rings:
            if db == 2:
                ring.swaps = {}
            ring.swaps[db] = ring.begin(db)

    def rows(i):
        return pl.ds(pl.multiple_of(lax.rem(me + i, 8) * 32, 32), 32)

    cols = pl.ds(pl.multiple_of(me * 1024, 1024), 1024)
    for i in (4, 3, 5, 2, 6, 1, 7):
        waits.append(wires.send(dq_ref.at[rows(i), :], gq_ref.at[:, cols], z_at[i]))
    own = wires.local(dq_ref.at[rows(0), :], gq_ref.at[:, cols])
    for ring in rings:
        ring.one()
    for ring in rings:
        ring.two()
    for i in range(2):
        for ring in rings:
            ring.three(i)
    for ring in rings:
        ring.join(0)
    for ring in rings:
        ring.four()
    for ring in rings:
        ring.five()
    rings[0].six(gk_ref, 1.0 / math.sqrt(128.0))
    rings[1].six(gv_ref, 1.0)
    for copy in waits:
        copy.wait_recv()
    own.wait()
    wires.finish_sends()


ANY = pl.BlockSpec(memory_space=pl.ANY)
VM = pl.BlockSpec(memory_space=pltpu.VMEM)
SM = pl.BlockSpec(memory_space=pltpu.SMEM)
DMA = pltpu.SemaphoreType.DMA


def spread(q, o, g, k, v):
    bf16 = jnp.bfloat16
    rows = jax.ShapeDtypeStruct((256, 1024), bf16)
    cache = jax.ShapeDtypeStruct((4, 4, 2, 512, 128), bf16)
    return pl.pallas_call(
        spread_kernel,
        out_shape=(rows, rows, jax.ShapeDtypeStruct((8, 8, 128), jnp.float32), cache, cache),
        in_specs=[ANY] * 5,
        out_specs=(ANY,) * 5,
        scratch_shapes=[
            pltpu.VMEM((32, 8192), bf16),
            pltpu.VMEM((32, 8192), bf16),
            pltpu.VMEM((8, 8, 128), jnp.float32),
            DMA((96,)),
            DMA((96,)),
            DMA((8,)),
        ],
        compiler_params=pltpu.CompilerParams(
            collective_id=0, has_side_effects=True, vmem_limit_bytes=16 * 2**20
        ),
    )(q, o, g, k, v)


def collect(dq, dk, dv):
    bf16 = jnp.bfloat16
    out = jax.ShapeDtypeStruct((512, 128), bf16)
    return pl.pallas_call(
        collect_kernel,
        out_shape=(jax.ShapeDtypeStruct((32, 8192), bf16), out, out),
        in_specs=[ANY] * 3,
        out_specs=(ANY, VM, VM),
        scratch_shapes=[
            pltpu.VMEM((4, 4, 512, 128), bf16),
            pltpu.VMEM((4, 4, 512, 128), bf16),
            pltpu.VMEM((4, 4, 512, 128), bf16),
            pltpu.VMEM((4, 4, 512, 128), bf16),
            pltpu.VMEM((2, 2, 512, 128), bf16),
            pltpu.VMEM((2, 2, 512, 128), bf16),
            pltpu.VMEM((2, 4, 512, 128), bf16),
            pltpu.VMEM((2, 4, 512, 128), bf16),
            pltpu.VMEM((3, 512, 128), bf16),
            pltpu.VMEM((3, 512, 128), bf16),
            DMA((64,)),
            DMA((64,)),
            DMA((16,)),
        ],
        compiler_params=pltpu.CompilerParams(
            collective_id=1, has_side_effects=True, vmem_limit_bytes=40 * 2**20
        ),
    )(dq, dk, dv)


def on_device(
    query_rows, attn_out, grad_out, logsumexp, key_cache, value_cache, block_lists, block_counts
):
    q, g, dp, kf, vf = spread(query_rows, attn_out, grad_out, key_cache[0], value_cache[0])
    blocks = (128, 128, 128)
    dq, dk, dv = grads(
        block_lists, block_counts, q, g, logsumexp, dp, kf.reshape(blocks), vf.reshape(blocks)
    )
    gq, gk, gv = collect(dq, dk.reshape(kf.shape), dv.reshape(vf.shape))
    return gq, gk[None], gv[None]


def solution(mesh):
    placed = (
        P(("seq", "kv"), None),
        P(("seq", "kv"), None),
        P(("seq", "kv"), None),
        P("kv", "seq"),
        P("kv", "seq", None),
        P("kv", "seq", None),
        P("kv", "seq", None),
        P("kv", "seq"),
    )
    return jax.shard_map(
        on_device,
        mesh=mesh,
        in_specs=placed,
        out_specs=(P(("seq", "kv"), None), P("kv", "seq", None), P("kv", "seq", None)),
        check_vma=False,
    )
```

```python
import math

import jax
import jax.numpy as jnp
from jax import lax
from jax.experimental import pallas as pl
from jax.experimental.pallas import tpu as pltpu
from jax.sharding import PartitionSpec as P

MESH = pl.DeviceIdType.MESH

G = 4
UNROLL = 4
BLK = 128
LOG2E = math.log2(math.e)


def grads_kernel(
    lists_hbm, counts_hbm, q_ref, do_ref, lse_hbm, dp_ref, k_ref, v_ref,
    dq_ref, dk_ref, dv_ref,
    acc, dqa, w1, w2, row_delta, row_lse, slot_a, slot_b, row_of, at_of, lists, counts, lse_ref, sem,
):
    scale = 1.0 / math.sqrt(128.0)
    f32, bf16 = jnp.float32, jnp.bfloat16

    copies = [
        pltpu.make_async_copy(src, dst, sem.at[i])
        for i, (src, dst) in enumerate(
            ((counts_hbm, counts), (lists_hbm, lists), (lse_hbm, lse_ref))
        )
    ]
    for copy in copies:
        copy.start()

    def zero(i, _):
        acc[i] = jnp.zeros((BLK, 2 * BLK), f32)
        return 0

    lax.fori_loop(0, 128, zero, 0, unroll=4)

    for copy in copies:
        copy.wait()

    def list_row(r, n):
        def put(g, n):
            row_of[n] = r
            at_of[n] = g * G
            return n + 1

        return lax.fori_loop(0, (counts[lax.rem(r, 2), r // 2] + (G - 1)) // G, put, n)

    for i in range(UNROLL):
        row_of[i] = 0
        at_of[i] = 32
    total = lax.fori_loop(0, 16, list_row, UNROLL)
    for i in range(3 * UNROLL):
        row_of[total + i] = 0
        at_of[total + i] = 32

    for qb in range(2):
        d = dp_ref[4 * qb]
        for s in range(1, 4):
            d = d + pltpu.roll(dp_ref[4 * qb + s], 32 * s, 1)
        l = lse_ref[:, qb * BLK : (qb + 1) * BLK] * LOG2E
        for h in range(8):
            row_delta[2 * h + qb] = d[h : h + 1]
            row_lse[2 * h + qb] = l[h : h + 1]
    blank = jnp.zeros((BLK, BLK), bf16)

    def place_of(r):
        h, qb = r // 2, lax.rem(r, 2)
        return (
            pl.ds(pl.multiple_of(qb * BLK, BLK), BLK),
            pl.ds(pl.multiple_of(h * BLK, BLK), BLK),
        )

    def diagonal(a, b):
        return jnp.concatenate(
            [jnp.concatenate([a, blank], axis=1), jnp.concatenate([blank, b], axis=1)], axis=0
        )

    def prepare(r, _):
        q = q_ref[place_of(r)]
        d = do_ref[place_of(r)]
        w1[r] = diagonal(q.T, d.T)
        w2[r] = diagonal(q, d)
        dqa[r] = jnp.zeros((BLK, BLK), f32)
        return 0

    lax.fori_loop(0, 16, prepare, 0, unroll=4)
    causal = lax.broadcasted_iota(jnp.int32, (BLK, BLK), 0) <= lax.broadcasted_iota(
        jnp.int32, (BLK, BLK), 1
    )

    def where_of(n):
        r, first = row_of[n], at_of[n]
        h, qb = r // 2, lax.rem(r, 2)
        blocks = [lists[h, qb, jnp.minimum(first + i, 31)] for i in range(G)]
        return r, first, counts[qb, h], blocks

    def score(n, slot):
        r, _, _, blocks = where_of(n)
        pairs = [jnp.concatenate([k_ref[b], v_ref[b]], axis=1) for b in blocks]
        slot[...] = jnp.dot(jnp.concatenate(pairs, axis=0), w1[r], preferred_element_type=f32)

    def terms(n, slot):
        r, first, count, blocks = where_of(n)
        delta = row_delta[r]
        lse = row_lse[r]
        grad_scores, halves = [], []
        for i in range(G):
            s = slot[i * BLK : (i + 1) * BLK, :BLK]
            grad_weights = slot[i * BLK : (i + 1) * BLK, BLK:]
            bias = jnp.where(first + i < count, lse, 1e30)
            p = jnp.exp2(s * (scale * LOG2E) - bias)
            if i == 0:
                p = jnp.where(causal | (first > 0), p, 0.0)
            ds = (p * (grad_weights - delta)).astype(bf16)
            grad_scores.append(ds)
            halves.append(jnp.concatenate([ds, p.astype(bf16)], axis=1))
        out = jnp.dot(jnp.concatenate(halves, axis=0), w2[r], preferred_element_type=f32)
        dq = jnp.dot(
            jnp.concatenate([k_ref[b].T for b in blocks], axis=1),
            jnp.concatenate(grad_scores, axis=0),
            preferred_element_type=f32,
        )
        return r, blocks, out, dq

    def half(e, write, read):
        for u in range(UNROLL):
            score(e + UNROLL + u, write.at[u])
        for r, blocks, out, dq in [terms(e + u, read.at[u]) for u in range(UNROLL)]:
            dqa[r] += dq
            for i in range(G):
                acc[blocks[i]] += out[i * BLK : (i + 1) * BLK]

    def some_groups(m, _):
        half(2 * m * UNROLL, slot_a, slot_b)
        half((2 * m + 1) * UNROLL, slot_b, slot_a)
        return 0

    for u in range(UNROLL):
        slot_b[u] = jnp.zeros((G * BLK, 2 * BLK), f32)
    halves_needed = (total - UNROLL + UNROLL - 1) // UNROLL + 1
    lax.fori_loop(0, (halves_needed + 1) // 2, some_groups, 0)

    def finish_block(i, _):
        a = acc[i]
        dk_ref[i] = a[:, :BLK].astype(bf16)
        dv_ref[i] = a[:, BLK:].astype(bf16)
        return 0

    lax.fori_loop(0, 128, finish_block, 0, unroll=4)

    def finish_row(r, _):
        dq_ref[place_of(r)] = (dqa[r] * scale).astype(bf16).T
        return 0

    lax.fori_loop(0, 16, finish_row, 0, unroll=4)


def grads(lists, counts, q, do, lse, dp, k, v):
    vm = pl.BlockSpec(memory_space=pltpu.VMEM)
    hbm = pl.BlockSpec(memory_space=pltpu.HBM)
    bf16, f32 = jnp.bfloat16, jnp.float32
    return pl.pallas_call(
        grads_kernel,
        out_shape=(
            jax.ShapeDtypeStruct((256, 1024), bf16),
            jax.ShapeDtypeStruct((128, 128, 128), bf16),
            jax.ShapeDtypeStruct((128, 128, 128), bf16),
        ),
        in_specs=[hbm, hbm, vm, vm, hbm, vm, vm, vm],
        out_specs=(vm, vm, vm),
        scratch_shapes=[
            pltpu.VMEM((128, BLK, 2 * BLK), f32),
            pltpu.VMEM((16, BLK, BLK), f32),
            pltpu.VMEM((16, 2 * BLK, 2 * BLK), bf16),
            pltpu.VMEM((16, 2 * BLK, 2 * BLK), bf16),
            pltpu.VMEM((16, 1, BLK), f32),
            pltpu.VMEM((16, 1, BLK), f32),
            pltpu.VMEM((UNROLL, G * BLK, 2 * BLK), f32),
            pltpu.VMEM((UNROLL, G * BLK, 2 * BLK), f32),
            pltpu.SMEM((528,), jnp.int32),
            pltpu.SMEM((528,), jnp.int32),
            pltpu.SMEM((8, 2, 32), jnp.int32),
            pltpu.SMEM((2, 8), jnp.int32),
            pltpu.VMEM((8, 256), f32),
            pltpu.SemaphoreType.DMA((3,)),
        ],
        compiler_params=pltpu.CompilerParams(vmem_limit_bytes=36 * 2**20),
    )(lists, counts, q, do, lse, dp, k, v)


class Wires:
    def __init__(self, send_sem, recv_sem, local_sem):
        self.send_sem, self.recv_sem, self.local_sem = send_sem, recv_sem, local_sem
        self.count = 0
        self.local_count = 0
        self.started = []

    def send(self, src, dst, device):
        i = self.count
        self.count += 1
        copy = pltpu.make_async_remote_copy(
            src_ref=src,
            dst_ref=dst,
            send_sem=self.send_sem.at[i],
            recv_sem=self.recv_sem.at[i],
            device_id=device,
            device_id_type=MESH,
        )
        copy.start()
        self.started.append(copy)
        return copy

    def local(self, src, dst):
        i = self.local_count
        self.local_count += 1
        copy = pltpu.make_async_copy(src, dst, self.local_sem.at[i])
        copy.start()
        return copy

    def finish_sends(self):
        for copy in self.started:
            copy.wait_send()


def greet(devices):
    barrier = pltpu.get_barrier_semaphore()
    for device in devices:
        pl.semaphore_signal(barrier, inc=1, device_id=device, device_id_type=MESH)
    pl.semaphore_wait(barrier, len(devices))


def place():
    s = lax.axis_index("seq")
    x, y, c = s // 8, lax.rem(s // 2, 4), lax.rem(s, 2)

    def at(dx, dy, other=0):
        core = c if other == 0 else 1 - c
        return {"seq": (lax.rem(x + dx + 4, 4) * 4 + lax.rem(y + dy + 4, 4)) * 2 + core}

    return x, y, c, at


def wrap4(i):
    return lax.rem(i + 4, 4)


def spread_kernel(
    q_ref, o_ref, g_ref, k_ref, v_ref,
    qo_ref, go_ref, dp_ref, kf_ref, vf_ref,
    o_buf, g_buf, d_buf, send_sem, recv_sem, local_sem,
):
    me = lax.axis_index("kv")
    x, y, c, at = place()
    z_at = [{"kv": lax.rem(me + i, 8)} for i in range(8)]
    greet(z_at[1:] + [at(1, 0), at(-1, 0), at(0, 1), at(0, -1), at(0, 0, 1)])
    wires = Wires(send_sem, recv_sem, local_sem)
    locals_ = []
    waits = []

    load_o = wires.local(o_ref, o_buf)
    load_g = wires.local(g_ref, g_buf)

    class Ring:
        def __init__(self, src, full, x_first):
            self.src, self.full, self.x_first = src, full, x_first

        def dev(self, da, db):
            return at(da, db) if self.x_first else at(db, da)

        def slot(self, da, db, half=None):
            dx, dy = (da, db) if self.x_first else (db, da)
            ref = self.full.at[wrap4(x + dx), wrap4(y + dy), c]
            return ref if half is None else ref.at[pl.ds(half * 256, 256)]

        def put(self, ref, da, db):
            return wires.send(ref, ref, self.dev(da, db))

        def share(self, da, db):
            ref = self.slot(da, db)
            waits.append(wires.send(ref, ref, at(0, 0, 1)))

        def begin(self):
            own = self.slot(0, 0)
            self.ap = wires.send(self.src, own, self.dev(1, 0))
            self.am = wires.send(self.src, own, self.dev(-1, 0))
            self.bp = [wires.send(self.src, own, self.dev(0, 1))]
            self.bm = [wires.send(self.src, own, self.dev(0, -1))]

        def own(self):
            own = self.slot(0, 0)
            waits.append(wires.send(self.src, own, at(0, 0, 1)))
            locals_.append(wires.local(self.src, own))

        def both(self, ref):
            self.bp.append(self.put(ref, 0, 1))
            self.bm.append(self.put(ref, 0, -1))

        def first(self):
            self.ap.wait_recv()
            self.a2p = self.put(self.slot(-1, 0, 0), 1, 0)
            self.both(self.slot(-1, 0))
            self.am.wait_recv()
            self.a2m = self.put(self.slot(1, 0, 1), -1, 0)
            self.both(self.slot(1, 0))
            self.share(-1, 0)
            self.share(1, 0)

        def second(self):
            self.a2p.wait_recv()
            self.both(self.slot(2, 0, 0))
            self.a2m.wait_recv()
            self.both(self.slot(2, 0, 1))
            self.share(2, 0)

        def third(self, step):
            if step == 0:
                self.bp[0].wait_recv()
                self.c = [self.put(self.slot(0, -1), 0, 1)]
                self.share(0, -1)
                self.bm[0].wait_recv()
                self.share(0, 1)
            elif step == 1:
                self.bp[1].wait_recv()
                self.c.append(self.put(self.slot(-1, -1), 0, 1))
                self.share(-1, -1)
                self.bm[1].wait_recv()
                self.share(-1, 1)
            elif step == 2:
                self.bp[2].wait_recv()
                self.share(1, -1)
                self.bm[2].wait_recv()
                self.c.append(self.put(self.slot(1, 1), 0, -1))
                self.share(1, 1)
            else:
                self.bm[3].wait_recv()
                self.c.append(self.put(self.slot(2, 1, 0), 0, -1))
                self.bm[4].wait_recv()
                self.c.append(self.put(self.slot(2, 1, 1), 0, -1))
                self.share(2, 1)
                self.bp[3].wait_recv()
                self.bp[4].wait_recv()
                self.share(2, -1)

        def fourth(self, step):
            if step < 3:
                self.c[step].wait_recv()
                self.share((0, -1, 1)[step], 2)
            else:
                self.c[3].wait_recv()
                self.c[4].wait_recv()
                self.share(2, 2)

    rings = (Ring(k_ref.at[0], kf_ref, True), Ring(v_ref.at[0], vf_ref, False))
    for ring in rings:
        ring.begin()
    rows = pl.ds(pl.multiple_of(me * 32, 32), 32)

    def columns(i):
        return pl.ds(pl.multiple_of(lax.rem(me + i, 8) * 1024, 1024), 1024)

    for i in (1, 7, 2, 6, 3, 5, 4):
        for src, dst in ((q_ref, qo_ref), (g_ref, go_ref)):
            waits.append(wires.send(src.at[:, columns(i)], dst.at[rows, :], z_at[i]))
    for src, dst in ((q_ref, qo_ref), (g_ref, go_ref)):
        locals_.append(wires.local(src.at[:, columns(0)], dst.at[rows, :]))
    for ring in rings:
        ring.own()

    load_o.wait()
    load_g.wait()
    of_head = (
        lax.broadcasted_iota(jnp.int32, (8, 1024), 1) // 128
        == lax.broadcasted_iota(jnp.int32, (8, 1024), 0)
    ).astype(jnp.float32)
    d_buf[...] = jnp.zeros(d_buf.shape, jnp.float32)
    for group in range(8):
        cols = pl.ds(group * 1024, 1024)
        terms = o_buf[:, cols].astype(jnp.float32) * g_buf[:, cols].astype(jnp.float32)
        d_buf[group, :, :32] = lax.dot_general(
            of_head,
            terms,
            (((1,), (1,)), ((), ())),
            precision=lax.Precision.HIGHEST,
            preferred_element_type=jnp.float32,
        )
    for i in range(1, 8):
        waits.append(wires.send(d_buf.at[lax.rem(me + i, 8)], dp_ref.at[me], z_at[i]))
    locals_.append(wires.local(d_buf.at[me], dp_ref.at[me]))

    for ring in rings:
        ring.first()
    for ring in rings:
        ring.second()
    for step in range(4):
        for ring in rings:
            ring.third(step)
    for step in range(4):
        for ring in rings:
            ring.fourth(step)
    for copy in waits:
        copy.wait_recv()
    for copy in locals_:
        copy.wait()
    wires.finish_sends()


def collect_kernel(
    dq_ref, dk_ref, dv_ref,
    gq_ref, gk_ref, gv_ref,
    mine_k, mine_v, sib_k, sib_v, far_k, far_v, near_k, near_v, end_k, end_v,
    send_sem, recv_sem, local_sem,
):
    me = lax.axis_index("kv")
    x, y, c, at = place()
    z_at = [{"kv": lax.rem(me + i, 8)} for i in range(8)]
    greet(z_at[1:] + [at(1, 0), at(-1, 0), at(0, 1), at(0, -1), at(0, 0, 1)])
    wires = Wires(send_sem, recv_sem, local_sem)
    f32, bf16 = jnp.float32, jnp.bfloat16
    waits = []
    lo, hi = pl.ds(0, 256), pl.ds(256, 256)
    order = (
        (2, 2), (-1, 2), (1, 2), (0, 2),
        (-1, 1), (2, -1), (1, -1),
        (2, 1), (-1, -1), (1, 1), (0, -1), (0, 1),
        (2, 0), (1, 0), (-1, 0), (0, 0),
    )

    class Ring:
        def __init__(self, src, mine, sib, far, near, end, x_first):
            self.src, self.mine, self.sib = src, mine, sib
            self.far, self.near, self.end, self.x_first = far, near, end, x_first
            self.swaps, self.fars, self.nears = {}, {}, {}

        def dev(self, da, db):
            return at(da, db) if self.x_first else at(db, da)

        def cell(self, ref, da, db):
            dx, dy = (da, db) if self.x_first else (db, da)
            return ref.at[wrap4(x + dx), wrap4(y + dy)]

        def swap(self, da, db):
            self.swaps[da, db] = wires.send(
                self.cell(self.src, da, db).at[1 - c], self.cell(self.sib, da, db), at(0, 0, 1)
            )

        def pair(self, da, db):
            self.swaps[da, db].wait_recv()
            here = self.cell(self.src, da, db).at[c]
            return here[...].astype(f32) + self.cell(self.sib, da, db)[...].astype(f32)

        def send(self, piece, da, db, dst, device):
            m = self.cell(self.mine, da, db)
            m[...] = piece.astype(bf16)
            return wires.send(m, dst, device)

        def to_far(self, da):
            up = da > 0
            side = 0 if up else 1
            i = (2, 1).index(da) if up else (-1, 0).index(da)
            self.fars[da] = self.send(
                self.pair(da, 2), da, 2, self.far.at[side, i], self.dev(0, 1 if up else -1)
            )

        def to_near(self, da, db):
            piece = self.pair(da, db)
            side = 0 if db == 1 else 1
            if (da > 0) == (db == 1):
                i = (2, 1).index(da) if da > 0 else (-1, 0).index(da)
                self.fars[da].wait_recv()
                piece = piece + self.far[side, i].astype(f32)
            self.nears[da, db] = self.send(
                piece, da, db, self.near.at[side, da % 4], self.dev(0, db)
            )

        def total(self, da):
            piece = self.pair(da, 0)
            self.nears[da, -1].wait_recv()
            piece = piece + self.near[1, da % 4].astype(f32)
            self.nears[da, 1].wait_recv()
            return piece + self.near[0, da % 4].astype(f32)

        def turn(self):
            m = self.cell(self.mine, 2, 0)
            m[...] = self.total(2).astype(bf16)
            self.end_far_p = wires.send(m.at[lo], self.end.at[0, lo], self.dev(1, 0))
            self.end_far_m = wires.send(m.at[hi], self.end.at[0, hi], self.dev(-1, 0))

        def side(self, da):
            m = self.cell(self.mine, da, 0)
            piece = self.total(da)
            if da == 1:
                m[hi] = piece[256:].astype(bf16)
                self.end_far_p.wait_recv()
                m[lo] = (piece[:256] + self.end[0, lo].astype(f32)).astype(bf16)
                self.end_p = wires.send(m, self.end.at[1], self.dev(1, 0))
            else:
                m[lo] = piece[:256].astype(bf16)
                self.end_far_m.wait_recv()
                m[hi] = (piece[256:] + self.end[0, hi].astype(f32)).astype(bf16)
                self.end_m = wires.send(m, self.end.at[2], self.dev(-1, 0))

        def last(self, out, scale):
            t = self.total(0)
            self.end_p.wait_recv()
            t = t + self.end[1].astype(f32)
            self.end_m.wait_recv()
            t = t + self.end[2].astype(f32)
            out[...] = (t * scale).astype(bf16)

    rings = (
        Ring(dk_ref, mine_k, sib_k, far_k, near_k, end_k, True),
        Ring(dv_ref, mine_v, sib_v, far_v, near_v, end_v, False),
    )
    for da, db in order:
        for ring in rings:
            ring.swap(da, db)

    def rows(i):
        return pl.ds(pl.multiple_of(lax.rem(me + i, 8) * 32, 32), 32)

    cols = pl.ds(pl.multiple_of(me * 1024, 1024), 1024)
    for i in (4, 3, 5, 2, 6, 1, 7):
        waits.append(wires.send(dq_ref.at[rows(i), :], gq_ref.at[:, cols], z_at[i]))
    own = wires.local(dq_ref.at[rows(0), :], gq_ref.at[:, cols])
    for da, db in order[:12]:
        for ring in rings:
            if db == 2:
                ring.to_far(da)
            else:
                ring.to_near(da, db)
    for ring in rings:
        ring.turn()
    for da in (1, -1):
        for ring in rings:
            ring.side(da)
    rings[0].last(gk_ref, 1.0 / math.sqrt(128.0))
    rings[1].last(gv_ref, 1.0)
    for copy in waits:
        copy.wait_recv()
    own.wait()
    wires.finish_sends()


ANY = pl.BlockSpec(memory_space=pl.ANY)
HBM = pl.BlockSpec(memory_space=pltpu.HBM)
VM = pl.BlockSpec(memory_space=pltpu.VMEM)
SM = pl.BlockSpec(memory_space=pltpu.SMEM)
DMA = pltpu.SemaphoreType.DMA


def spread(q, o, g, k, v):
    bf16 = jnp.bfloat16
    rows = jax.ShapeDtypeStruct((256, 1024), bf16)
    cache = jax.ShapeDtypeStruct((4, 4, 2, 512, 128), bf16)
    return pl.pallas_call(
        spread_kernel,
        out_shape=(rows, rows, jax.ShapeDtypeStruct((8, 8, 128), jnp.float32), cache, cache),
        in_specs=[HBM] * 5,
        out_specs=(ANY,) * 5,
        scratch_shapes=[
            pltpu.VMEM((32, 8192), bf16),
            pltpu.VMEM((32, 8192), bf16),
            pltpu.VMEM((8, 8, 128), jnp.float32),
            DMA((96,)),
            DMA((96,)),
            DMA((8,)),
        ],
        compiler_params=pltpu.CompilerParams(
            collective_id=0, has_side_effects=True, vmem_limit_bytes=4 * 2**20
        ),
    )(q, o, g, k, v)


def collect(dq, dk, dv):
    bf16 = jnp.bfloat16
    out = jax.ShapeDtypeStruct((512, 128), bf16)
    return pl.pallas_call(
        collect_kernel,
        out_shape=(jax.ShapeDtypeStruct((32, 8192), bf16), out, out),
        in_specs=[ANY, VM, VM],
        out_specs=(ANY, VM, VM),
        scratch_shapes=[
            pltpu.VMEM((4, 4, 512, 128), bf16),
            pltpu.VMEM((4, 4, 512, 128), bf16),
            pltpu.VMEM((4, 4, 512, 128), bf16),
            pltpu.VMEM((4, 4, 512, 128), bf16),
            pltpu.VMEM((2, 2, 512, 128), bf16),
            pltpu.VMEM((2, 2, 512, 128), bf16),
            pltpu.VMEM((2, 4, 512, 128), bf16),
            pltpu.VMEM((2, 4, 512, 128), bf16),
            pltpu.VMEM((3, 512, 128), bf16),
            pltpu.VMEM((3, 512, 128), bf16),
            DMA((72,)),
            DMA((72,)),
            DMA((1,)),
        ],
        compiler_params=pltpu.CompilerParams(
            collective_id=1, has_side_effects=True, vmem_limit_bytes=20 * 2**20
        ),
    )(dq, dk, dv)


def on_device(
    query_rows, attn_out, grad_out, logsumexp, key_cache, value_cache, block_lists, block_counts
):
    def stay(a):
        return pltpu.with_memory_space_constraint(a, pltpu.HBM)

    q, g, dp, kf, vf = spread(
        stay(query_rows), stay(attn_out), stay(grad_out), stay(key_cache), stay(value_cache)
    )
    blocks = (128, 128, 128)
    dq, dk, dv = grads(
        stay(block_lists),
        stay(block_counts.T),
        q,
        g,
        stay(logsumexp),
        dp,
        kf.reshape(blocks),
        vf.reshape(blocks),
    )
    gq, gk, gv = collect(dq, dk.reshape(kf.shape), dv.reshape(vf.shape))
    return gq, gk[None], gv[None]


def solution(mesh):
    placed = (
        P(("seq", "kv"), None),
        P(("seq", "kv"), None),
        P(("seq", "kv"), None),
        P("kv", "seq"),
        P("kv", "seq", None),
        P("kv", "seq", None),
        P("kv", "seq", None),
        P("kv", "seq"),
    )
    return jax.shard_map(
        on_device,
        mesh=mesh,
        in_specs=placed,
        out_specs=(P(("seq", "kv"), None), P("kv", "seq", None), P("kv", "seq", None)),
        check_vma=False,
    )
```

```python
import math

import jax
import jax.numpy as jnp
from jax import lax
from jax.experimental import pallas as pl
from jax.experimental.pallas import tpu as pltpu
from jax.sharding import PartitionSpec as P

MESH = pl.DeviceIdType.MESH

G = 4
UNROLL = 4
BLK = 128
LOG2E = math.log2(math.e)


def grads_kernel(
    lists_hbm, counts_hbm, q_ref, do_ref, lse_hbm, dp_ref, k_ref, v_ref,
    dq_ref, dk_ref, dv_ref,
    acc, dqa, w1, w2, row_delta, row_lse, slot_a, slot_b, row_of, at_of, lists, counts, lse_ref, sem,
):
    scale = 1.0 / math.sqrt(128.0)
    f32, bf16 = jnp.float32, jnp.bfloat16

    copies = [
        pltpu.make_async_copy(src, dst, sem.at[i])
        for i, (src, dst) in enumerate(
            ((counts_hbm, counts), (lists_hbm, lists), (lse_hbm, lse_ref))
        )
    ]
    for copy in copies:
        copy.start()

    def zero(i, _):
        acc[i] = jnp.zeros((BLK, 2 * BLK), f32)
        return 0

    lax.fori_loop(0, 128, zero, 0, unroll=4)

    for copy in copies:
        copy.wait()

    def list_row(r, n):
        def put(g, n):
            row_of[n] = r
            at_of[n] = g * G
            return n + 1

        return lax.fori_loop(0, (counts[lax.rem(r, 2), r // 2] + (G - 1)) // G, put, n)

    total = lax.fori_loop(0, 16, list_row, 0)
    for i in range(2 * UNROLL):
        row_of[total + i] = 0
        at_of[total + i] = 32

    for qb in range(2):
        d = dp_ref[4 * qb]
        for s in range(1, 4):
            d = d + pltpu.roll(dp_ref[4 * qb + s], 32 * s, 1)
        l = lse_ref[:, qb * BLK : (qb + 1) * BLK] * LOG2E
        for h in range(8):
            row_delta[2 * h + qb] = d[h : h + 1]
            row_lse[2 * h + qb] = l[h : h + 1]
    blank = jnp.zeros((BLK, BLK), bf16)

    def place_of(r):
        h, qb = r // 2, lax.rem(r, 2)
        return (
            pl.ds(pl.multiple_of(qb * BLK, BLK), BLK),
            pl.ds(pl.multiple_of(h * BLK, BLK), BLK),
        )

    def diagonal(a, b):
        return jnp.concatenate(
            [jnp.concatenate([a, blank], axis=1), jnp.concatenate([blank, b], axis=1)], axis=0
        )

    def prepare(r, _):
        q = q_ref[place_of(r)]
        d = do_ref[place_of(r)]
        w1[r] = diagonal(q.T, d.T)
        w2[r] = diagonal(q, d)
        dqa[r] = jnp.zeros((BLK, BLK), f32)
        return 0

    lax.fori_loop(0, 16, prepare, 0, unroll=4)
    causal = lax.broadcasted_iota(jnp.int32, (BLK, BLK), 0) <= lax.broadcasted_iota(
        jnp.int32, (BLK, BLK), 1
    )

    def where_of(n):
        r, first = row_of[n], at_of[n]
        h, qb = r // 2, lax.rem(r, 2)
        blocks = [lists[h, qb, jnp.minimum(first + i, 31)] for i in range(G)]
        return r, first, counts[qb, h], blocks

    def score(n, slot):
        r, _, _, blocks = where_of(n)
        pairs = [jnp.concatenate([k_ref[b], v_ref[b]], axis=1) for b in blocks]
        slot[...] = jnp.dot(jnp.concatenate(pairs, axis=0), w1[r], preferred_element_type=f32)

    def terms(n, slot):
        r, first, count, blocks = where_of(n)
        delta = row_delta[r]
        lse = row_lse[r]
        grad_scores, halves = [], []
        for i in range(G):
            s = slot[i * BLK : (i + 1) * BLK, :BLK]
            grad_weights = slot[i * BLK : (i + 1) * BLK, BLK:]
            bias = jnp.where(first + i < count, lse, 1e30)
            p = jnp.exp2(s * (scale * LOG2E) - bias)
            if i == 0:
                p = jnp.where(causal | (first > 0), p, 0.0)
            ds = (p * (grad_weights - delta)).astype(bf16)
            grad_scores.append(ds)
            halves.append(jnp.concatenate([ds, p.astype(bf16)], axis=1))
        out = jnp.dot(jnp.concatenate(halves, axis=0), w2[r], preferred_element_type=f32)
        dq = jnp.dot(
            jnp.concatenate([k_ref[b].T for b in blocks], axis=1),
            jnp.concatenate(grad_scores, axis=0),
            preferred_element_type=f32,
        )
        return r, blocks, out, dq

    def score_step(k, write):
        for u in range(UNROLL):
            score(k * UNROLL + u, write.at[u])

    def step(k, write, read):
        score_step(k + 1, write)
        for r, blocks, out, dq in [terms(k * UNROLL + u, read.at[u]) for u in range(UNROLL)]:
            dqa[r] += dq
            for i in range(G):
                acc[blocks[i]] += out[i * BLK : (i + 1) * BLK]

    steps = (total + UNROLL - 1) // UNROLL

    def two_steps(m, _):
        step(2 * m, slot_b, slot_a)

        @pl.when(2 * m + 1 < steps)
        def _():
            step(2 * m + 1, slot_a, slot_b)

        return 0

    score_step(0, slot_a)
    lax.fori_loop(0, (steps + 1) // 2, two_steps, 0)

    def finish_block(i, _):
        a = acc[i]
        dk_ref[i] = a[:, :BLK].astype(bf16)
        dv_ref[i] = a[:, BLK:].astype(bf16)
        return 0

    lax.fori_loop(0, 128, finish_block, 0, unroll=4)

    def finish_row(r, _):
        dq_ref[place_of(r)] = (dqa[r] * scale).astype(bf16).T
        return 0

    lax.fori_loop(0, 16, finish_row, 0, unroll=4)


def grads(lists, counts, q, do, lse, dp, k, v):
    vm = pl.BlockSpec(memory_space=pltpu.VMEM)
    hbm = pl.BlockSpec(memory_space=pltpu.HBM)
    bf16, f32 = jnp.bfloat16, jnp.float32
    return pl.pallas_call(
        grads_kernel,
        out_shape=(
            jax.ShapeDtypeStruct((256, 1024), bf16),
            jax.ShapeDtypeStruct((128, 128, 128), bf16),
            jax.ShapeDtypeStruct((128, 128, 128), bf16),
        ),
        in_specs=[hbm, hbm, vm, vm, hbm, vm, vm, vm],
        out_specs=(vm, vm, vm),
        scratch_shapes=[
            pltpu.VMEM((128, BLK, 2 * BLK), f32),
            pltpu.VMEM((16, BLK, BLK), f32),
            pltpu.VMEM((16, 2 * BLK, 2 * BLK), bf16),
            pltpu.VMEM((16, 2 * BLK, 2 * BLK), bf16),
            pltpu.VMEM((16, 1, BLK), f32),
            pltpu.VMEM((16, 1, BLK), f32),
            pltpu.VMEM((UNROLL, G * BLK, 2 * BLK), f32),
            pltpu.VMEM((UNROLL, G * BLK, 2 * BLK), f32),
            pltpu.SMEM((528,), jnp.int32),
            pltpu.SMEM((528,), jnp.int32),
            pltpu.SMEM((8, 2, 32), jnp.int32),
            pltpu.SMEM((2, 8), jnp.int32),
            pltpu.VMEM((8, 256), f32),
            pltpu.SemaphoreType.DMA((3,)),
        ],
        compiler_params=pltpu.CompilerParams(vmem_limit_bytes=36 * 2**20),
    )(lists, counts, q, do, lse, dp, k, v)


class Wires:
    def __init__(self, send_sem, recv_sem, local_sem):
        self.send_sem, self.recv_sem, self.local_sem = send_sem, recv_sem, local_sem
        self.count = 0
        self.local_count = 0
        self.started = []

    def send(self, src, dst, device):
        i = self.count
        self.count += 1
        copy = pltpu.make_async_remote_copy(
            src_ref=src,
            dst_ref=dst,
            send_sem=self.send_sem.at[i],
            recv_sem=self.recv_sem.at[i],
            device_id=device,
            device_id_type=MESH,
        )
        copy.start()
        self.started.append(copy)
        return copy

    def local(self, src, dst):
        i = self.local_count
        self.local_count += 1
        copy = pltpu.make_async_copy(src, dst, self.local_sem.at[i])
        copy.start()
        return copy

    def finish_sends(self):
        for copy in self.started:
            copy.wait_send()


def greet(devices):
    barrier = pltpu.get_barrier_semaphore()
    for device in devices:
        pl.semaphore_signal(barrier, inc=1, device_id=device, device_id_type=MESH)
    pl.semaphore_wait(barrier, len(devices))


def place():
    s = lax.axis_index("seq")
    x, y, c = s // 8, lax.rem(s // 2, 4), lax.rem(s, 2)

    def at(dx, dy, other=0):
        core = c if other == 0 else 1 - c
        return {"seq": (lax.rem(x + dx + 4, 4) * 4 + lax.rem(y + dy + 4, 4)) * 2 + core}

    return x, y, c, at


SLOTS = ((1, 4), (1, 3), (1, 2), (2, 4), (2, 3), (3, 4))


def wrap4(i):
    return lax.rem(i + 4, 4)


def spread_kernel(
    q_ref, o_ref, g_ref, k_ref, v_ref,
    qo_ref, go_ref, dp_ref, kf_ref, vf_ref,
    o_buf, g_buf, d_buf, relay, d_relay, send_sem, recv_sem, local_sem,
):
    me = lax.axis_index("kv")
    x, y, c, at = place()
    z_at = {sign: {"kv": lax.rem(me + 8 + sign, 8)} for sign in (1, -1)}
    greet([z_at[1], z_at[-1], at(1, 0), at(-1, 0), at(0, 1), at(0, -1), at(0, 0, 1)])
    wires = Wires(send_sem, recv_sem, local_sem)
    locals_ = []
    waits = []

    load_o = wires.local(o_ref, o_buf)
    load_g = wires.local(g_ref, g_buf)

    class Ring:
        def __init__(self, src, full, x_first):
            self.src, self.full, self.x_first = src, full, x_first

        def dev(self, da, db):
            return at(da, db) if self.x_first else at(db, da)

        def slot(self, da, db, half=None):
            dx, dy = (da, db) if self.x_first else (db, da)
            ref = self.full.at[wrap4(x + dx), wrap4(y + dy), c]
            return ref if half is None else ref.at[pl.ds(half * 256, 256)]

        def put(self, ref, da, db):
            return wires.send(ref, ref, self.dev(da, db))

        def share(self, da, db):
            ref = self.slot(da, db)
            waits.append(wires.send(ref, ref, at(0, 0, 1)))

        def begin(self):
            own = self.slot(0, 0)
            self.ap = wires.send(self.src, own, self.dev(1, 0))
            self.am = wires.send(self.src, own, self.dev(-1, 0))
            self.bp = [wires.send(self.src, own, self.dev(0, 1))]
            self.bm = [wires.send(self.src, own, self.dev(0, -1))]

        def own(self):
            own = self.slot(0, 0)
            waits.append(wires.send(self.src, own, at(0, 0, 1)))
            locals_.append(wires.local(self.src, own))

        def both(self, ref):
            self.bp.append(self.put(ref, 0, 1))
            self.bm.append(self.put(ref, 0, -1))

        def first(self):
            self.ap.wait_recv()
            self.a2p = self.put(self.slot(-1, 0, 0), 1, 0)
            self.both(self.slot(-1, 0))
            self.am.wait_recv()
            self.a2m = self.put(self.slot(1, 0, 1), -1, 0)
            self.both(self.slot(1, 0))
            self.share(-1, 0)
            self.share(1, 0)

        def second(self):
            self.a2p.wait_recv()
            self.both(self.slot(2, 0, 0))
            self.a2m.wait_recv()
            self.both(self.slot(2, 0, 1))
            self.share(2, 0)

        def third(self, step):
            if step == 0:
                self.bp[0].wait_recv()
                self.c = [self.put(self.slot(0, -1), 0, 1)]
                self.share(0, -1)
                self.bm[0].wait_recv()
                self.share(0, 1)
            elif step == 1:
                self.bp[1].wait_recv()
                self.c.append(self.put(self.slot(-1, -1), 0, 1))
                self.share(-1, -1)
                self.bm[1].wait_recv()
                self.share(-1, 1)
            elif step == 2:
                self.bp[2].wait_recv()
                self.share(1, -1)
                self.bm[2].wait_recv()
                self.c.append(self.put(self.slot(1, 1), 0, -1))
                self.share(1, 1)
            else:
                self.bm[3].wait_recv()
                self.c.append(self.put(self.slot(2, 1, 0), 0, -1))
                self.bm[4].wait_recv()
                self.c.append(self.put(self.slot(2, 1, 1), 0, -1))
                self.share(2, 1)
                self.bp[3].wait_recv()
                self.bp[4].wait_recv()
                self.share(2, -1)

        def fourth(self, step):
            if step < 3:
                self.c[step].wait_recv()
                self.share((0, -1, 1)[step], 2)
            else:
                self.c[3].wait_recv()
                self.c[4].wait_recv()
                self.share(2, 2)

    rings = (Ring(k_ref.at[0], kf_ref, True), Ring(v_ref.at[0], vf_ref, False))
    for ring in rings:
        ring.begin()
    rows = pl.ds(pl.multiple_of(me * 32, 32), 32)

    def columns(i):
        return pl.ds(pl.multiple_of(lax.rem(me + i, 8) * 1024, 1024), 1024)

    moved = {}

    def z_hop(hop, far):
        for a, (src, dst) in enumerate(((q_ref, qo_ref), (g_ref, go_ref))):
            for side, sign in enumerate((1, -1)):
                first, count = (16 * side, 16) if far == 4 else (0, 32)
                if hop == 1:
                    part = src.at[pl.ds(first, count), columns(8 + sign * far)]
                else:
                    moved[a, side, hop - 1, far].wait_recv()
                    part = relay.at[a, side, SLOTS.index((hop - 1, far)), pl.ds(0, count)]
                if hop == far:
                    start = lax.rem(me + 8 - sign * (hop - 1), 8) * 32 + first
                    there = dst.at[pl.ds(pl.multiple_of(start, 16), count), :]
                else:
                    there = relay.at[a, side, SLOTS.index((hop, far)), pl.ds(0, count)]
                copy = wires.send(part, there, z_at[sign])
                moved[a, side, hop, far] = copy
                if hop == far:
                    waits.append(copy)

    def delta_hop(hop, far):
        for side, sign in enumerate((1, -1) if far < 4 else (1,)):
            if hop == 1:
                part = d_buf.at[lax.rem(me + 8 + sign * far, 8)]
            else:
                moved[2, side, hop - 1, far].wait_recv()
                part = d_relay.at[side, SLOTS.index((hop - 1, far))]
            if hop == far:
                there = dp_ref.at[lax.rem(me + 8 - sign * (hop - 1), 8)]
            else:
                there = d_relay.at[side, SLOTS.index((hop, far))]
            copy = wires.send(part, there, z_at[sign])
            moved[2, side, hop, far] = copy
            if hop == far:
                waits.append(copy)

    for far in (4, 3):
        z_hop(1, far)
    for src, dst in ((q_ref, qo_ref), (g_ref, go_ref)):
        locals_.append(wires.local(src.at[:, columns(0)], dst.at[rows, :]))
    for ring in rings:
        ring.own()

    load_o.wait()
    load_g.wait()
    of_head = (
        lax.broadcasted_iota(jnp.int32, (8, 1024), 1) // 128
        == lax.broadcasted_iota(jnp.int32, (8, 1024), 0)
    ).astype(jnp.float32)
    d_buf[...] = jnp.zeros(d_buf.shape, jnp.float32)
    for group in range(8):
        cols = pl.ds(group * 1024, 1024)
        terms = o_buf[:, cols].astype(jnp.float32) * g_buf[:, cols].astype(jnp.float32)
        d_buf[group, :, :32] = lax.dot_general(
            of_head,
            terms,
            (((1,), (1,)), ((), ())),
            precision=lax.Precision.HIGHEST,
            preferred_element_type=jnp.float32,
        )
    for far in (4, 3, 2, 1):
        delta_hop(1, far)
    for far in (2, 1):
        z_hop(1, far)
    locals_.append(wires.local(d_buf.at[me], dp_ref.at[me]))

    for ring in rings:
        ring.first()
    for far in (4, 3, 2):
        z_hop(2, far)
        delta_hop(2, far)
    for ring in rings:
        ring.second()
    for step in range(2):
        for ring in rings:
            ring.third(step)
    for far in (4, 3):
        z_hop(3, far)
        delta_hop(3, far)
    for step in range(2, 4):
        for ring in rings:
            ring.third(step)
    z_hop(4, 4)
    delta_hop(4, 4)
    for step in range(4):
        for ring in rings:
            ring.fourth(step)
    for copy in waits:
        copy.wait_recv()
    for copy in locals_:
        copy.wait()
    wires.finish_sends()


def collect_kernel(
    dq_ref, dk_ref, dv_ref,
    gq_ref, gk_ref, gv_ref,
    mine_k, mine_v, sib_k, sib_v, far_k, far_v, near_k, near_v, end_k, end_v, relay,
    send_sem, recv_sem, local_sem,
):
    me = lax.axis_index("kv")
    x, y, c, at = place()
    z_at = {sign: {"kv": lax.rem(me + 8 + sign, 8)} for sign in (1, -1)}
    greet([z_at[1], z_at[-1], at(1, 0), at(-1, 0), at(0, 1), at(0, -1), at(0, 0, 1)])
    wires = Wires(send_sem, recv_sem, local_sem)
    f32, bf16 = jnp.float32, jnp.bfloat16
    waits = []
    lo, hi = pl.ds(0, 256), pl.ds(256, 256)
    order = (
        (2, 2), (-1, 2), (1, 2), (0, 2),
        (-1, 1), (2, -1), (1, -1),
        (2, 1), (-1, -1), (1, 1), (0, -1), (0, 1),
        (2, 0), (1, 0), (-1, 0), (0, 0),
    )

    class Ring:
        def __init__(self, src, mine, sib, far, near, end, x_first):
            self.src, self.mine, self.sib = src, mine, sib
            self.far, self.near, self.end, self.x_first = far, near, end, x_first
            self.swaps, self.fars, self.nears = {}, {}, {}

        def dev(self, da, db):
            return at(da, db) if self.x_first else at(db, da)

        def cell(self, ref, da, db):
            dx, dy = (da, db) if self.x_first else (db, da)
            return ref.at[wrap4(x + dx), wrap4(y + dy)]

        def swap(self, da, db):
            self.swaps[da, db] = wires.send(
                self.cell(self.src, da, db).at[1 - c], self.cell(self.sib, da, db), at(0, 0, 1)
            )

        def pair(self, da, db):
            self.swaps[da, db].wait_recv()
            here = self.cell(self.src, da, db).at[c]
            return here[...].astype(f32) + self.cell(self.sib, da, db)[...].astype(f32)

        def send(self, piece, da, db, dst, device):
            m = self.cell(self.mine, da, db)
            m[...] = piece.astype(bf16)
            return wires.send(m, dst, device)

        def to_far(self, da):
            up = da > 0
            side = 0 if up else 1
            i = (2, 1).index(da) if up else (-1, 0).index(da)
            self.fars[da] = self.send(
                self.pair(da, 2), da, 2, self.far.at[side, i], self.dev(0, 1 if up else -1)
            )

        def to_near(self, da, db):
            piece = self.pair(da, db)
            side = 0 if db == 1 else 1
            if (da > 0) == (db == 1):
                i = (2, 1).index(da) if da > 0 else (-1, 0).index(da)
                self.fars[da].wait_recv()
                piece = piece + self.far[side, i].astype(f32)
            self.nears[da, db] = self.send(
                piece, da, db, self.near.at[side, da % 4], self.dev(0, db)
            )

        def total(self, da):
            piece = self.pair(da, 0)
            self.nears[da, -1].wait_recv()
            piece = piece + self.near[1, da % 4].astype(f32)
            self.nears[da, 1].wait_recv()
            return piece + self.near[0, da % 4].astype(f32)

        def turn(self):
            m = self.cell(self.mine, 2, 0)
            m[...] = self.total(2).astype(bf16)
            self.end_far_p = wires.send(m.at[lo], self.end.at[0, lo], self.dev(1, 0))
            self.end_far_m = wires.send(m.at[hi], self.end.at[0, hi], self.dev(-1, 0))

        def side(self, da):
            m = self.cell(self.mine, da, 0)
            piece = self.total(da)
            if da == 1:
                m[hi] = piece[256:].astype(bf16)
                self.end_far_p.wait_recv()
                m[lo] = (piece[:256] + self.end[0, lo].astype(f32)).astype(bf16)
                self.end_p = wires.send(m, self.end.at[1], self.dev(1, 0))
            else:
                m[lo] = piece[:256].astype(bf16)
                self.end_far_m.wait_recv()
                m[hi] = (piece[256:] + self.end[0, hi].astype(f32)).astype(bf16)
                self.end_m = wires.send(m, self.end.at[2], self.dev(-1, 0))

        def last(self, out, scale):
            t = self.total(0)
            self.end_p.wait_recv()
            t = t + self.end[1].astype(f32)
            self.end_m.wait_recv()
            t = t + self.end[2].astype(f32)
            out[...] = (t * scale).astype(bf16)

    rings = (
        Ring(dk_ref, mine_k, sib_k, far_k, near_k, end_k, True),
        Ring(dv_ref, mine_v, sib_v, far_v, near_v, end_v, False),
    )
    for da, db in order:
        for ring in rings:
            ring.swap(da, db)

    def columns(i):
        return pl.ds(pl.multiple_of(lax.rem(me + 8 + i, 8) * 1024, 1024), 1024)

    moved = {}

    def z_hop(hop, far):
        for side, sign in enumerate((1, -1)):
            first, count = (16 * side, 16) if far == 4 else (0, 32)
            if hop == 1:
                start = lax.rem(me + 8 + sign * far, 8) * 32 + first
                part = dq_ref.at[pl.ds(pl.multiple_of(start, 16), count), :]
            else:
                moved[side, hop - 1, far].wait_recv()
                part = relay.at[side, SLOTS.index((hop - 1, far)), pl.ds(0, count)]
            if hop == far:
                there = gq_ref.at[pl.ds(first, count), columns(-sign * (hop - 1))]
            else:
                there = relay.at[side, SLOTS.index((hop, far)), pl.ds(0, count)]
            copy = wires.send(part, there, z_at[sign])
            moved[side, hop, far] = copy
            if hop == far:
                waits.append(copy)

    for far in (4, 3, 2, 1):
        z_hop(1, far)
    mine = pl.ds(pl.multiple_of(me * 32, 32), 32)
    own = wires.local(dq_ref.at[mine, :], gq_ref.at[:, columns(0)])
    for step, (da, db) in enumerate(order[:12]):
        for ring in rings:
            if db == 2:
                ring.to_far(da)
            else:
                ring.to_near(da, db)
        if step == 7:
            for far in (4, 3, 2):
                z_hop(2, far)
    for far in (4, 3):
        z_hop(3, far)
    for ring in rings:
        ring.turn()
    z_hop(4, 4)
    for da in (1, -1):
        for ring in rings:
            ring.side(da)
    rings[0].last(gk_ref, 1.0 / math.sqrt(128.0))
    rings[1].last(gv_ref, 1.0)
    for copy in waits:
        copy.wait_recv()
    own.wait()
    wires.finish_sends()


ANY = pl.BlockSpec(memory_space=pl.ANY)
HBM = pl.BlockSpec(memory_space=pltpu.HBM)
VM = pl.BlockSpec(memory_space=pltpu.VMEM)
SM = pl.BlockSpec(memory_space=pltpu.SMEM)
DMA = pltpu.SemaphoreType.DMA


def spread(q, o, g, k, v):
    bf16 = jnp.bfloat16
    rows = jax.ShapeDtypeStruct((256, 1024), bf16)
    cache = jax.ShapeDtypeStruct((4, 4, 2, 512, 128), bf16)
    return pl.pallas_call(
        spread_kernel,
        out_shape=(rows, rows, jax.ShapeDtypeStruct((8, 8, 128), jnp.float32), cache, cache),
        in_specs=[HBM] * 5,
        out_specs=(ANY,) * 5,
        scratch_shapes=[
            pltpu.VMEM((32, 8192), bf16),
            pltpu.VMEM((32, 8192), bf16),
            pltpu.VMEM((8, 8, 128), jnp.float32),
            pltpu.VMEM((2, 2, 6, 32, 1024), bf16),
            pltpu.VMEM((2, 6, 8, 128), jnp.float32),
            DMA((144,)),
            DMA((144,)),
            DMA((8,)),
        ],
        compiler_params=pltpu.CompilerParams(
            collective_id=0, has_side_effects=True, vmem_limit_bytes=4 * 2**20
        ),
    )(q, o, g, k, v)


def collect(dq, dk, dv):
    bf16 = jnp.bfloat16
    out = jax.ShapeDtypeStruct((512, 128), bf16)
    return pl.pallas_call(
        collect_kernel,
        out_shape=(jax.ShapeDtypeStruct((32, 8192), bf16), out, out),
        in_specs=[ANY, VM, VM],
        out_specs=(ANY, VM, VM),
        scratch_shapes=[
            pltpu.VMEM((4, 4, 512, 128), bf16),
            pltpu.VMEM((4, 4, 512, 128), bf16),
            pltpu.VMEM((4, 4, 512, 128), bf16),
            pltpu.VMEM((4, 4, 512, 128), bf16),
            pltpu.VMEM((2, 2, 512, 128), bf16),
            pltpu.VMEM((2, 2, 512, 128), bf16),
            pltpu.VMEM((2, 4, 512, 128), bf16),
            pltpu.VMEM((2, 4, 512, 128), bf16),
            pltpu.VMEM((3, 512, 128), bf16),
            pltpu.VMEM((3, 512, 128), bf16),
            pltpu.VMEM((2, 6, 32, 1024), bf16),
            DMA((96,)),
            DMA((96,)),
            DMA((1,)),
        ],
        compiler_params=pltpu.CompilerParams(
            collective_id=1, has_side_effects=True, vmem_limit_bytes=20 * 2**20
        ),
    )(dq, dk, dv)


def on_device(
    query_rows, attn_out, grad_out, logsumexp, key_cache, value_cache, block_lists, block_counts
):
    def stay(a):
        return pltpu.with_memory_space_constraint(a, pltpu.HBM)

    q, g, dp, kf, vf = spread(
        stay(query_rows), stay(attn_out), stay(grad_out), stay(key_cache), stay(value_cache)
    )
    blocks = (128, 128, 128)
    dq, dk, dv = grads(
        stay(block_lists),
        stay(block_counts.T),
        q,
        g,
        stay(logsumexp),
        dp,
        kf.reshape(blocks),
        vf.reshape(blocks),
    )
    gq, gk, gv = collect(dq, dk.reshape(kf.shape), dv.reshape(vf.shape))
    return gq, gk[None], gv[None]


def solution(mesh):
    placed = (
        P(("seq", "kv"), None),
        P(("seq", "kv"), None),
        P(("seq", "kv"), None),
        P("kv", "seq"),
        P("kv", "seq", None),
        P("kv", "seq", None),
        P("kv", "seq", None),
        P("kv", "seq"),
    )
    return jax.shard_map(
        on_device,
        mesh=mesh,
        in_specs=placed,
        out_specs=(P(("seq", "kv"), None), P("kv", "seq", None), P("kv", "seq", None)),
        check_vma=False,
    )
```

```python
import math

import jax
import jax.numpy as jnp
from jax import lax
from jax.experimental import pallas as pl
from jax.experimental.pallas import tpu as pltpu
from jax.sharding import PartitionSpec as P

MESH = pl.DeviceIdType.MESH

G = 4
UNROLL = 4
BLK = 128
LOG2E = math.log2(math.e)


def grads_kernel(
    lists_hbm, counts_hbm, q_ref, do_ref, lse_hbm, dp_ref, k_ref, v_ref,
    dq_ref, dk_ref, dv_ref,
    acc, dqa, w1, w2, row_delta, row_lse, slot_a, slot_b, row_of, at_of, lists, counts, lse_ref, sem,
):
    scale = 1.0 / math.sqrt(128.0)
    f32, bf16 = jnp.float32, jnp.bfloat16

    copies = [
        pltpu.make_async_copy(src, dst, sem.at[i])
        for i, (src, dst) in enumerate(
            ((counts_hbm, counts), (lists_hbm, lists), (lse_hbm, lse_ref))
        )
    ]
    for copy in copies:
        copy.start()

    def zero(i, _):
        acc[i] = jnp.zeros((BLK, 2 * BLK), f32)
        return 0

    lax.fori_loop(0, 128, zero, 0, unroll=4)

    blank = jnp.zeros((BLK, BLK), bf16)

    def place_of(r):
        h, qb = r // 2, lax.rem(r, 2)
        return (
            pl.ds(pl.multiple_of(qb * BLK, BLK), BLK),
            pl.ds(pl.multiple_of(h * BLK, BLK), BLK),
        )

    def diagonal(a, b):
        return jnp.concatenate(
            [jnp.concatenate([a, blank], axis=1), jnp.concatenate([blank, b], axis=1)], axis=0
        )

    def prepare(r, _):
        q = q_ref[place_of(r)]
        d = do_ref[place_of(r)]
        w1[r] = diagonal(q.T, d.T)
        w2[r] = diagonal(q, d)
        dqa[r] = jnp.zeros((BLK, BLK), f32)
        return 0

    lax.fori_loop(0, 16, prepare, 0, unroll=4)
    for copy in copies:
        copy.wait()

    total = jnp.int32(0)
    for r in range(16):
        for g in range(32 // G):
            row_of[total + g] = r
            at_of[total + g] = g * G
        total = total + (counts[r % 2, r // 2] + (G - 1)) // G
    for i in range(2 * UNROLL):
        row_of[total + i] = 0
        at_of[total + i] = 32

    for qb in range(2):
        d = dp_ref[4 * qb]
        for s in range(1, 4):
            d = d + pltpu.roll(dp_ref[4 * qb + s], 32 * s, 1)
        l = lse_ref[:, qb * BLK : (qb + 1) * BLK] * LOG2E
        for h in range(8):
            row_delta[2 * h + qb] = d[h : h + 1]
            row_lse[2 * h + qb] = l[h : h + 1]
    causal = lax.broadcasted_iota(jnp.int32, (BLK, BLK), 0) <= lax.broadcasted_iota(
        jnp.int32, (BLK, BLK), 1
    )

    def where_of(n):
        r, first = row_of[n], at_of[n]
        h, qb = r // 2, lax.rem(r, 2)
        blocks = [lists[h, qb, jnp.minimum(first + i, 31)] for i in range(G)]
        return r, first, counts[qb, h], blocks

    def score(n, slot):
        r, _, _, blocks = where_of(n)
        pairs = [jnp.concatenate([k_ref[b], v_ref[b]], axis=1) for b in blocks]
        slot[...] = jnp.dot(jnp.concatenate(pairs, axis=0), w1[r], preferred_element_type=f32)

    def terms(n, slot):
        r, first, count, blocks = where_of(n)
        delta = row_delta[r]
        lse = row_lse[r]
        grad_scores, halves = [], []
        for i in range(G):
            s = slot[i * BLK : (i + 1) * BLK, :BLK]
            grad_weights = slot[i * BLK : (i + 1) * BLK, BLK:]
            bias = jnp.where(first + i < count, lse, 1e30)
            p = jnp.exp2(s * (scale * LOG2E) - bias)
            if i == 0:
                p = jnp.where(causal | (first > 0), p, 0.0)
            ds = (p * (grad_weights - delta)).astype(bf16)
            grad_scores.append(ds)
            halves.append(jnp.concatenate([ds, p.astype(bf16)], axis=1))
        out = jnp.dot(jnp.concatenate(halves, axis=0), w2[r], preferred_element_type=f32)
        dq = jnp.dot(
            jnp.concatenate([k_ref[b].T for b in blocks], axis=1),
            jnp.concatenate(grad_scores, axis=0),
            preferred_element_type=f32,
        )
        return r, blocks, out, dq

    def score_step(k, write):
        for u in range(UNROLL):
            score(k * UNROLL + u, write.at[u])

    def step(k, write, read):
        score_step(k + 1, write)
        for r, blocks, out, dq in [terms(k * UNROLL + u, read.at[u]) for u in range(UNROLL)]:
            dqa[r] += dq
            for i in range(G):
                acc[blocks[i]] += out[i * BLK : (i + 1) * BLK]

    steps = (total + UNROLL - 1) // UNROLL

    def two_steps(m, _):
        step(2 * m, slot_b, slot_a)

        @pl.when(2 * m + 1 < steps)
        def _():
            step(2 * m + 1, slot_a, slot_b)

        return 0

    score_step(0, slot_a)
    lax.fori_loop(0, (steps + 1) // 2, two_steps, 0)

    def finish_block(i, _):
        a = acc[i]
        dk_ref[i] = a[:, :BLK].astype(bf16)
        dv_ref[i] = a[:, BLK:].astype(bf16)
        return 0

    lax.fori_loop(0, 128, finish_block, 0, unroll=4)

    def finish_row(r, _):
        dq_ref[place_of(r)] = (dqa[r] * scale).astype(bf16).T
        return 0

    lax.fori_loop(0, 16, finish_row, 0, unroll=4)


def grads(lists, counts, q, do, lse, dp, k, v):
    vm = pl.BlockSpec(memory_space=pltpu.VMEM)
    hbm = pl.BlockSpec(memory_space=pltpu.HBM)
    bf16, f32 = jnp.bfloat16, jnp.float32
    return pl.pallas_call(
        grads_kernel,
        out_shape=(
            jax.ShapeDtypeStruct((256, 1024), bf16),
            jax.ShapeDtypeStruct((128, 128, 128), bf16),
            jax.ShapeDtypeStruct((128, 128, 128), bf16),
        ),
        in_specs=[hbm, hbm, vm, vm, hbm, vm, vm, vm],
        out_specs=(vm, vm, vm),
        scratch_shapes=[
            pltpu.VMEM((128, BLK, 2 * BLK), f32),
            pltpu.VMEM((16, BLK, BLK), f32),
            pltpu.VMEM((16, 2 * BLK, 2 * BLK), bf16),
            pltpu.VMEM((16, 2 * BLK, 2 * BLK), bf16),
            pltpu.VMEM((16, 1, BLK), f32),
            pltpu.VMEM((16, 1, BLK), f32),
            pltpu.VMEM((UNROLL, G * BLK, 2 * BLK), f32),
            pltpu.VMEM((UNROLL, G * BLK, 2 * BLK), f32),
            pltpu.SMEM((528,), jnp.int32),
            pltpu.SMEM((528,), jnp.int32),
            pltpu.SMEM((8, 2, 32), jnp.int32),
            pltpu.SMEM((2, 8), jnp.int32),
            pltpu.VMEM((8, 256), f32),
            pltpu.SemaphoreType.DMA((3,)),
        ],
        compiler_params=pltpu.CompilerParams(vmem_limit_bytes=36 * 2**20),
    )(lists, counts, q, do, lse, dp, k, v)


class Wires:
    def __init__(self, send_sem, recv_sem, local_sem):
        self.send_sem, self.recv_sem, self.local_sem = send_sem, recv_sem, local_sem
        self.count = 0
        self.local_count = 0
        self.started = []

    def send(self, src, dst, device):
        i = self.count
        self.count += 1
        copy = pltpu.make_async_remote_copy(
            src_ref=src,
            dst_ref=dst,
            send_sem=self.send_sem.at[i],
            recv_sem=self.recv_sem.at[i],
            device_id=device,
            device_id_type=MESH,
        )
        copy.start()
        self.started.append(copy)
        return copy

    def local(self, src, dst):
        i = self.local_count
        self.local_count += 1
        copy = pltpu.make_async_copy(src, dst, self.local_sem.at[i])
        copy.start()
        return copy

    def finish_sends(self):
        for copy in self.started:
            copy.wait_send()


def greet(devices):
    barrier = pltpu.get_barrier_semaphore()
    for device in devices:
        pl.semaphore_signal(barrier, inc=1, device_id=device, device_id_type=MESH)
    pl.semaphore_wait(barrier, len(devices))


def place():
    s = lax.axis_index("seq")
    x, y, c = s // 8, lax.rem(s // 2, 4), lax.rem(s, 2)

    def at(dx, dy, other=0):
        core = c if other == 0 else 1 - c
        return {"seq": (lax.rem(x + dx + 4, 4) * 4 + lax.rem(y + dy + 4, 4)) * 2 + core}

    return x, y, c, at


SLOTS = ((1, 4), (1, 3), (1, 2), (2, 4), (2, 3), (3, 4))


def wrap4(i):
    return lax.rem(i + 4, 4)


def spread_kernel(
    q_ref, o_ref, g_ref, k_ref, v_ref,
    qo_ref, go_ref, dp_ref, kf_ref, vf_ref,
    o_buf, g_buf, d_buf, relay, d_relay, send_sem, recv_sem, local_sem,
):
    me = lax.axis_index("kv")
    x, y, c, at = place()
    z_at = {sign: {"kv": lax.rem(me + 8 + sign, 8)} for sign in (1, -1)}
    greet([z_at[1], z_at[-1], at(1, 0), at(-1, 0), at(0, 1), at(0, -1), at(0, 0, 1)])
    wires = Wires(send_sem, recv_sem, local_sem)
    locals_ = []
    waits = []

    load_o = wires.local(o_ref, o_buf)
    load_g = wires.local(g_ref, g_buf)

    class Ring:
        def __init__(self, src, full, x_first):
            self.src, self.full, self.x_first = src, full, x_first

        def dev(self, da, db):
            return at(da, db) if self.x_first else at(db, da)

        def slot(self, da, db, half=None):
            dx, dy = (da, db) if self.x_first else (db, da)
            ref = self.full.at[wrap4(x + dx), wrap4(y + dy), c]
            return ref if half is None else ref.at[pl.ds(half * 256, 256)]

        def put(self, ref, da, db):
            return wires.send(ref, ref, self.dev(da, db))

        def share(self, da, db):
            ref = self.slot(da, db)
            waits.append(wires.send(ref, ref, at(0, 0, 1)))

        def begin(self):
            own = self.slot(0, 0)
            self.ap = wires.send(self.src, own, self.dev(1, 0))
            self.am = wires.send(self.src, own, self.dev(-1, 0))
            self.bp = [wires.send(self.src, own, self.dev(0, 1))]
            self.bm = [wires.send(self.src, own, self.dev(0, -1))]

        def own(self):
            own = self.slot(0, 0)
            waits.append(wires.send(self.src, own, at(0, 0, 1)))
            locals_.append(wires.local(self.src, own))

        def both(self, ref):
            self.bp.append(self.put(ref, 0, 1))
            self.bm.append(self.put(ref, 0, -1))

        def first(self):
            self.ap.wait_recv()
            self.a2p = self.put(self.slot(-1, 0, 0), 1, 0)
            self.both(self.slot(-1, 0))
            self.am.wait_recv()
            self.a2m = self.put(self.slot(1, 0, 1), -1, 0)
            self.both(self.slot(1, 0))
            self.share(-1, 0)
            self.share(1, 0)

        def second(self):
            self.a2p.wait_recv()
            self.both(self.slot(2, 0, 0))
            self.a2m.wait_recv()
            self.both(self.slot(2, 0, 1))
            self.share(2, 0)

        def third(self, step):
            if step == 0:
                self.bp[0].wait_recv()
                self.c = [self.put(self.slot(0, -1), 0, 1)]
                self.share(0, -1)
                self.bm[0].wait_recv()
                self.share(0, 1)
            elif step == 1:
                self.bp[1].wait_recv()
                self.c.append(self.put(self.slot(-1, -1), 0, 1))
                self.share(-1, -1)
                self.bm[1].wait_recv()
                self.share(-1, 1)
            elif step == 2:
                self.bp[2].wait_recv()
                self.share(1, -1)
                self.bm[2].wait_recv()
                self.c.append(self.put(self.slot(1, 1), 0, -1))
                self.share(1, 1)
            else:
                self.bm[3].wait_recv()
                self.c.append(self.put(self.slot(2, 1, 0), 0, -1))
                self.bm[4].wait_recv()
                self.c.append(self.put(self.slot(2, 1, 1), 0, -1))
                self.share(2, 1)
                self.bp[3].wait_recv()
                self.bp[4].wait_recv()
                self.share(2, -1)

        def fourth(self, step):
            if step < 3:
                self.c[step].wait_recv()
                self.share((0, -1, 1)[step], 2)
            else:
                self.c[3].wait_recv()
                self.c[4].wait_recv()
                self.share(2, 2)

    rings = (Ring(k_ref.at[0], kf_ref, True), Ring(v_ref.at[0], vf_ref, False))
    for ring in rings:
        ring.begin()
    rows = pl.ds(pl.multiple_of(me * 32, 32), 32)

    def columns(i):
        return pl.ds(pl.multiple_of(lax.rem(me + i, 8) * 1024, 1024), 1024)

    moved = {}

    def z_hop(hop, far):
        for a, (src, dst) in enumerate(((q_ref, qo_ref), (g_ref, go_ref))):
            for side, sign in enumerate((1, -1)):
                first, count = (16 * side, 16) if far == 4 else (0, 32)
                if hop == 1:
                    part = src.at[pl.ds(first, count), columns(8 + sign * far)]
                else:
                    moved[a, side, hop - 1, far].wait_recv()
                    part = relay.at[a, side, SLOTS.index((hop - 1, far)), pl.ds(0, count)]
                if hop == far:
                    start = lax.rem(me + 8 - sign * (hop - 1), 8) * 32 + first
                    there = dst.at[pl.ds(pl.multiple_of(start, 16), count), :]
                else:
                    there = relay.at[a, side, SLOTS.index((hop, far)), pl.ds(0, count)]
                copy = wires.send(part, there, z_at[sign])
                moved[a, side, hop, far] = copy
                if hop == far:
                    waits.append(copy)

    def delta_hop(hop, far):
        for side, sign in enumerate((1, -1) if far < 4 else (1,)):
            if hop == 1:
                part = d_buf.at[lax.rem(me + 8 + sign * far, 8)]
            else:
                moved[2, side, hop - 1, far].wait_recv()
                part = d_relay.at[side, SLOTS.index((hop - 1, far))]
            if hop == far:
                there = dp_ref.at[lax.rem(me + 8 - sign * (hop - 1), 8)]
            else:
                there = d_relay.at[side, SLOTS.index((hop, far))]
            copy = wires.send(part, there, z_at[sign])
            moved[2, side, hop, far] = copy
            if hop == far:
                waits.append(copy)

    for far in (4, 3, 2):
        z_hop(1, far)
    for src, dst in ((q_ref, qo_ref), (g_ref, go_ref)):
        locals_.append(wires.local(src.at[:, columns(0)], dst.at[rows, :]))
    for ring in rings:
        ring.own()

    load_o.wait()
    load_g.wait()
    of_head = (
        lax.broadcasted_iota(jnp.int32, (8, 1024), 1) // 128
        == lax.broadcasted_iota(jnp.int32, (8, 1024), 0)
    ).astype(jnp.float32)
    d_buf[...] = jnp.zeros(d_buf.shape, jnp.float32)
    for group in range(8):
        cols = pl.ds(group * 1024, 1024)
        terms = o_buf[:, cols].astype(jnp.float32) * g_buf[:, cols].astype(jnp.float32)
        d_buf[group, :, :32] = lax.dot_general(
            of_head,
            terms,
            (((1,), (1,)), ((), ())),
            precision=lax.Precision.HIGHEST,
            preferred_element_type=jnp.float32,
        )
    for far in (4, 3, 2, 1):
        delta_hop(1, far)
    z_hop(1, 1)
    locals_.append(wires.local(d_buf.at[me], dp_ref.at[me]))

    for ring in rings:
        ring.first()
    for far in (4, 3, 2):
        z_hop(2, far)
        delta_hop(2, far)
    for ring in rings:
        ring.second()
    for step in range(2):
        for ring in rings:
            ring.third(step)
    for far in (4, 3):
        z_hop(3, far)
        delta_hop(3, far)
    for step in range(2, 4):
        for ring in rings:
            ring.third(step)
    z_hop(4, 4)
    delta_hop(4, 4)
    for step in (0, 2, 1, 3):
        for ring in rings:
            ring.fourth(step)
    for copy in waits:
        copy.wait_recv()
    for copy in locals_:
        copy.wait()
    wires.finish_sends()


def collect_kernel(
    dq_ref, dk_ref, dv_ref,
    gq_ref, gkv_ref,
    mine_k, mine_v, sib_k, sib_v, far_k, far_v, near_k, near_v, end_k, end_v, relay,
    send_sem, recv_sem, local_sem,
):
    me = lax.axis_index("kv")
    x, y, c, at = place()
    z_at = {sign: {"kv": lax.rem(me + 8 + sign, 8)} for sign in (1, -1)}
    greet([z_at[1], z_at[-1], at(1, 0), at(-1, 0), at(0, 1), at(0, -1), at(0, 0, 1)])
    wires = Wires(send_sem, recv_sem, local_sem)
    f32, bf16 = jnp.float32, jnp.bfloat16
    waits = []
    lo, hi = pl.ds(0, 256), pl.ds(256, 256)
    order = (
        (2, 2), (-1, 2), (1, 2), (0, 2),
        (-1, 1), (2, -1), (1, -1),
        (2, 1), (-1, -1), (1, 1), (0, -1), (0, 1),
        (2, 0), (1, 0), (-1, 0), (0, 0),
    )

    class Ring:
        def __init__(self, src, mine, sib, far, near, end, x_first):
            self.src, self.mine, self.sib = src, mine, sib
            self.far, self.near, self.end, self.x_first = far, near, end, x_first
            self.swaps, self.fars, self.nears = {}, {}, {}

        def dev(self, da, db):
            return at(da, db) if self.x_first else at(db, da)

        def cell(self, ref, da, db):
            dx, dy = (da, db) if self.x_first else (db, da)
            return ref.at[wrap4(x + dx), wrap4(y + dy)]

        def swap(self, da, db):
            self.swaps[da, db] = wires.send(
                self.cell(self.src, da, db).at[1 - c], self.cell(self.sib, da, db), at(0, 0, 1)
            )

        def pair(self, da, db):
            self.swaps[da, db].wait_recv()
            here = self.cell(self.src, da, db).at[c]
            return here[...].astype(f32) + self.cell(self.sib, da, db)[...].astype(f32)

        def send(self, piece, da, db, dst, device):
            m = self.cell(self.mine, da, db)
            m[...] = piece.astype(bf16)
            return wires.send(m, dst, device)

        def to_far(self, da):
            up = da > 0
            side = 0 if up else 1
            i = (2, 1).index(da) if up else (-1, 0).index(da)
            self.fars[da] = self.send(
                self.pair(da, 2), da, 2, self.far.at[side, i], self.dev(0, 1 if up else -1)
            )

        def to_near(self, da, db):
            piece = self.pair(da, db)
            side = 0 if db == 1 else 1
            if (da > 0) == (db == 1):
                i = (2, 1).index(da) if da > 0 else (-1, 0).index(da)
                self.fars[da].wait_recv()
                piece = piece + self.far[side, i].astype(f32)
            self.nears[da, db] = self.send(
                piece, da, db, self.near.at[side, da % 4], self.dev(0, db)
            )

        def total(self, da):
            piece = self.pair(da, 0)
            self.nears[da, -1].wait_recv()
            piece = piece + self.near[1, da % 4].astype(f32)
            self.nears[da, 1].wait_recv()
            return piece + self.near[0, da % 4].astype(f32)

        def turn(self):
            m = self.cell(self.mine, 2, 0)
            m[...] = self.total(2).astype(bf16)
            self.end_far_p = wires.send(m.at[lo], self.end.at[0, lo], self.dev(1, 0))
            self.end_far_m = wires.send(m.at[hi], self.end.at[0, hi], self.dev(-1, 0))

        def side(self, da):
            m = self.cell(self.mine, da, 0)
            piece = self.total(da)
            if da == 1:
                m[hi] = piece[256:].astype(bf16)
                self.end_far_p.wait_recv()
                m[lo] = (piece[:256] + self.end[0, lo].astype(f32)).astype(bf16)
                self.end_p = wires.send(m, self.end.at[1], self.dev(1, 0))
            else:
                m[lo] = piece[:256].astype(bf16)
                self.end_far_m.wait_recv()
                m[hi] = (piece[256:] + self.end[0, hi].astype(f32)).astype(bf16)
                self.end_m = wires.send(m, self.end.at[2], self.dev(-1, 0))

        def last(self, out, scale):
            t = self.total(0)
            self.end_p.wait_recv()
            t = t + self.end[1].astype(f32)
            self.end_m.wait_recv()
            t = t + self.end[2].astype(f32)
            out[...] = (t * scale).astype(bf16)

    rings = (
        Ring(dk_ref, mine_k, sib_k, far_k, near_k, end_k, True),
        Ring(dv_ref, mine_v, sib_v, far_v, near_v, end_v, False),
    )
    for da, db in order:
        for ring in rings:
            ring.swap(da, db)

    def columns(i):
        return pl.ds(pl.multiple_of(lax.rem(me + 8 + i, 8) * 1024, 1024), 1024)

    moved = {}

    def z_hop(hop, far):
        for side, sign in enumerate((1, -1)):
            first, count = (16 * side, 16) if far == 4 else (0, 32)
            if hop == 1:
                start = lax.rem(me + 8 + sign * far, 8) * 32 + first
                part = dq_ref.at[pl.ds(pl.multiple_of(start, 16), count), :]
            else:
                moved[side, hop - 1, far].wait_recv()
                part = relay.at[side, SLOTS.index((hop - 1, far)), pl.ds(0, count)]
            if hop == far:
                there = gq_ref.at[pl.ds(first, count), columns(-sign * (hop - 1))]
            else:
                there = relay.at[side, SLOTS.index((hop, far)), pl.ds(0, count)]
            copy = wires.send(part, there, z_at[sign])
            moved[side, hop, far] = copy
            if hop == far:
                waits.append(copy)

    for far in (4, 3, 2, 1):
        z_hop(1, far)
    mine = pl.ds(pl.multiple_of(me * 32, 32), 32)
    own = wires.local(dq_ref.at[mine, :], gq_ref.at[:, columns(0)])
    for step, (da, db) in enumerate(order[:12]):
        for ring in rings:
            if db == 2:
                ring.to_far(da)
            else:
                ring.to_near(da, db)
        if step == 7:
            for far in (4, 3, 2):
                z_hop(2, far)
    for far in (4, 3):
        z_hop(3, far)
    for ring in rings:
        ring.turn()
    z_hop(4, 4)
    for da in (1, -1):
        for ring in rings:
            ring.side(da)
    rings[0].last(gkv_ref.at[0], 1.0 / math.sqrt(128.0))
    rings[1].last(gkv_ref.at[1], 1.0)
    for copy in waits:
        copy.wait_recv()
    own.wait()
    wires.finish_sends()


ANY = pl.BlockSpec(memory_space=pl.ANY)
HBM = pl.BlockSpec(memory_space=pltpu.HBM)
VM = pl.BlockSpec(memory_space=pltpu.VMEM)
SM = pl.BlockSpec(memory_space=pltpu.SMEM)
DMA = pltpu.SemaphoreType.DMA


def spread(q, o, g, k, v):
    bf16 = jnp.bfloat16
    rows = jax.ShapeDtypeStruct((256, 1024), bf16)
    cache = jax.ShapeDtypeStruct((4, 4, 2, 512, 128), bf16)
    return pl.pallas_call(
        spread_kernel,
        out_shape=(rows, rows, jax.ShapeDtypeStruct((8, 8, 128), jnp.float32), cache, cache),
        in_specs=[HBM] * 5,
        out_specs=(ANY,) * 5,
        scratch_shapes=[
            pltpu.VMEM((32, 8192), bf16),
            pltpu.VMEM((32, 8192), bf16),
            pltpu.VMEM((8, 8, 128), jnp.float32),
            pltpu.VMEM((2, 2, 6, 32, 1024), bf16),
            pltpu.VMEM((2, 6, 8, 128), jnp.float32),
            DMA((144,)),
            DMA((144,)),
            DMA((8,)),
        ],
        compiler_params=pltpu.CompilerParams(
            collective_id=0, has_side_effects=True, vmem_limit_bytes=4 * 2**20
        ),
    )(q, o, g, k, v)


def collect(dq, dk, dv):
    bf16 = jnp.bfloat16
    out = jax.ShapeDtypeStruct((2, 512, 128), bf16)
    return pl.pallas_call(
        collect_kernel,
        out_shape=(jax.ShapeDtypeStruct((32, 8192), bf16), out),
        in_specs=[ANY, VM, VM],
        out_specs=(ANY, VM),
        scratch_shapes=[
            pltpu.VMEM((4, 4, 512, 128), bf16),
            pltpu.VMEM((4, 4, 512, 128), bf16),
            pltpu.VMEM((4, 4, 512, 128), bf16),
            pltpu.VMEM((4, 4, 512, 128), bf16),
            pltpu.VMEM((2, 2, 512, 128), bf16),
            pltpu.VMEM((2, 2, 512, 128), bf16),
            pltpu.VMEM((2, 4, 512, 128), bf16),
            pltpu.VMEM((2, 4, 512, 128), bf16),
            pltpu.VMEM((3, 512, 128), bf16),
            pltpu.VMEM((3, 512, 128), bf16),
            pltpu.VMEM((2, 6, 32, 1024), bf16),
            DMA((96,)),
            DMA((96,)),
            DMA((1,)),
        ],
        compiler_params=pltpu.CompilerParams(
            collective_id=1, has_side_effects=True, vmem_limit_bytes=20 * 2**20
        ),
    )(dq, dk, dv)


def on_device(
    query_rows, attn_out, grad_out, logsumexp, key_cache, value_cache, block_lists, block_counts
):
    def stay(a):
        return pltpu.with_memory_space_constraint(a, pltpu.HBM)

    q, g, dp, kf, vf = spread(
        stay(query_rows), stay(attn_out), stay(grad_out), stay(key_cache), stay(value_cache)
    )
    blocks = (128, 128, 128)
    dq, dk, dv = grads(
        stay(block_lists),
        stay(block_counts.T),
        q,
        g,
        stay(logsumexp),
        dp,
        kf.reshape(blocks),
        vf.reshape(blocks),
    )
    gq, pair = collect(dq, dk.reshape(kf.shape), dv.reshape(vf.shape))
    return gq, pair[:1], pair[1:]


def solution(mesh):
    placed = (
        P(("seq", "kv"), None),
        P(("seq", "kv"), None),
        P(("seq", "kv"), None),
        P("kv", "seq"),
        P("kv", "seq", None),
        P("kv", "seq", None),
        P("kv", "seq", None),
        P("kv", "seq"),
    )
    return jax.shard_map(
        on_device,
        mesh=mesh,
        in_specs=placed,
        out_specs=(P(("seq", "kv"), None), P("kv", "seq", None), P("kv", "seq", None)),
        check_vma=False,
    )
```

```python
import math

import jax
import jax.numpy as jnp
from jax import lax
from jax.experimental import pallas as pl
from jax.experimental.pallas import tpu as pltpu
from jax.sharding import PartitionSpec as P

MESH = pl.DeviceIdType.MESH

G = 4
UNROLL = 4
BLK = 128
LOG2E = math.log2(math.e)


def grads_kernel(
    lists_hbm, counts_hbm, q_ref, do_ref, lse_hbm, dp_ref, k_ref, v_ref,
    dq_ref, acc,
    dqa, w1, w2, row_delta, row_lse, slot_a, slot_b, row_of, at_of, lists, counts, lse_ref, sem,
):
    scale = 1.0 / math.sqrt(128.0)
    f32, bf16 = jnp.float32, jnp.bfloat16

    copies = [
        pltpu.make_async_copy(src, dst, sem.at[i])
        for i, (src, dst) in enumerate(
            ((counts_hbm, counts), (lists_hbm, lists), (lse_hbm, lse_ref))
        )
    ]
    for copy in copies:
        copy.start()

    def zero(i, _):
        acc[i] = jnp.zeros((BLK, 2 * BLK), f32)
        return 0

    lax.fori_loop(0, 128, zero, 0, unroll=4)

    blank = jnp.zeros((BLK, BLK), bf16)

    def place_of(r):
        h, qb = r // 2, lax.rem(r, 2)
        return (
            pl.ds(pl.multiple_of(qb * BLK, BLK), BLK),
            pl.ds(pl.multiple_of(h * BLK, BLK), BLK),
        )

    def diagonal(a, b):
        return jnp.concatenate(
            [jnp.concatenate([a, blank], axis=1), jnp.concatenate([blank, b], axis=1)], axis=0
        )

    def prepare(r, _):
        q = q_ref[place_of(r)]
        d = do_ref[place_of(r)]
        w1[r] = diagonal(q.T, d.T)
        w2[r] = diagonal(q, d)
        dqa[r] = jnp.zeros((BLK, BLK), f32)
        return 0

    lax.fori_loop(0, 16, prepare, 0, unroll=8)
    for copy in copies:
        copy.wait()

    total = jnp.int32(0)
    for r in range(16):
        for g in range(32 // G):
            row_of[total + g] = r
            at_of[total + g] = g * G
        total = total + (counts[r % 2, r // 2] + (G - 1)) // G
    for i in range(2 * UNROLL):
        row_of[total + i] = 0
        at_of[total + i] = 32

    for qb in range(2):
        d = dp_ref[4 * qb]
        for s in range(1, 4):
            d = d + pltpu.roll(dp_ref[4 * qb + s], 32 * s, 1)
        l = lse_ref[:, qb * BLK : (qb + 1) * BLK] * LOG2E
        for h in range(8):
            row_delta[2 * h + qb] = d[h : h + 1]
            row_lse[2 * h + qb] = l[h : h + 1]
    causal = lax.broadcasted_iota(jnp.int32, (BLK, BLK), 0) <= lax.broadcasted_iota(
        jnp.int32, (BLK, BLK), 1
    )

    def where_of(n):
        r, first = row_of[n], at_of[n]
        h, qb = r // 2, lax.rem(r, 2)
        blocks = [lists[h, qb, jnp.minimum(first + i, 31)] for i in range(G)]
        return r, first, counts[qb, h], blocks

    def score(n, slot):
        r, _, _, blocks = where_of(n)
        pairs = [jnp.concatenate([k_ref[b], v_ref[b]], axis=1) for b in blocks]
        slot[...] = jnp.dot(jnp.concatenate(pairs, axis=0), w1[r], preferred_element_type=f32)

    def terms(n, slot):
        r, first, count, blocks = where_of(n)
        delta = row_delta[r]
        lse = row_lse[r]
        grad_scores, halves = [], []
        for i in range(G):
            s = slot[i * BLK : (i + 1) * BLK, :BLK]
            grad_weights = slot[i * BLK : (i + 1) * BLK, BLK:]
            bias = jnp.where(first + i < count, lse, 1e30)
            p = jnp.exp2(s * (scale * LOG2E) - bias)
            if i == 0:
                p = jnp.where(causal | (first > 0), p, 0.0)
            ds = (p * (grad_weights - delta)).astype(bf16)
            grad_scores.append(ds)
            halves.append(jnp.concatenate([ds, p.astype(bf16)], axis=1))
        out = jnp.dot(jnp.concatenate(halves, axis=0), w2[r], preferred_element_type=f32)
        dq = jnp.dot(
            jnp.concatenate([k_ref[b].T for b in blocks], axis=1),
            jnp.concatenate(grad_scores, axis=0),
            preferred_element_type=f32,
        )
        return r, blocks, out, dq

    def score_step(k, write):
        for u in range(UNROLL):
            score(k * UNROLL + u, write.at[u])

    def step(k, write, read):
        score_step(k + 1, write)
        for r, blocks, out, dq in [terms(k * UNROLL + u, read.at[u]) for u in range(UNROLL)]:
            dqa[r] += dq
            for i in range(G):
                acc[blocks[i]] += out[i * BLK : (i + 1) * BLK]

    steps = (total + UNROLL - 1) // UNROLL

    def two_steps(m, _):
        step(2 * m, slot_b, slot_a)

        @pl.when(2 * m + 1 < steps)
        def _():
            step(2 * m + 1, slot_a, slot_b)

        return 0

    score_step(0, slot_a)
    lax.fori_loop(0, (steps + 1) // 2, two_steps, 0)

    def finish_row(r, _):
        dq_ref[place_of(r)] = (dqa[r] * scale).astype(bf16).T
        return 0

    lax.fori_loop(0, 16, finish_row, 0, unroll=8)


def grads(lists, counts, q, do, lse, dp, k, v):
    vm = pl.BlockSpec(memory_space=pltpu.VMEM)
    hbm = pl.BlockSpec(memory_space=pltpu.HBM)
    bf16, f32 = jnp.bfloat16, jnp.float32
    return pl.pallas_call(
        grads_kernel,
        out_shape=(
            jax.ShapeDtypeStruct((256, 1024), bf16),
            jax.ShapeDtypeStruct((128, BLK, 2 * BLK), f32),
        ),
        in_specs=[hbm, hbm, vm, vm, hbm, vm, vm, vm],
        out_specs=(vm, vm),
        scratch_shapes=[
            pltpu.VMEM((16, BLK, BLK), f32),
            pltpu.VMEM((16, 2 * BLK, 2 * BLK), bf16),
            pltpu.VMEM((16, 2 * BLK, 2 * BLK), bf16),
            pltpu.VMEM((16, 1, BLK), f32),
            pltpu.VMEM((16, 1, BLK), f32),
            pltpu.VMEM((UNROLL, G * BLK, 2 * BLK), f32),
            pltpu.VMEM((UNROLL, G * BLK, 2 * BLK), f32),
            pltpu.SMEM((528,), jnp.int32),
            pltpu.SMEM((528,), jnp.int32),
            pltpu.SMEM((8, 2, 32), jnp.int32),
            pltpu.SMEM((2, 8), jnp.int32),
            pltpu.VMEM((8, 256), f32),
            pltpu.SemaphoreType.DMA((3,)),
        ],
        compiler_params=pltpu.CompilerParams(vmem_limit_bytes=22 * 2**20),
    )(lists, counts, q, do, lse, dp, k, v)


class Wires:
    def __init__(self, send_sem, recv_sem, local_sem):
        self.send_sem, self.recv_sem, self.local_sem = send_sem, recv_sem, local_sem
        self.count = 0
        self.local_count = 0
        self.started = []

    def send(self, src, dst, device):
        i = self.count
        self.count += 1
        copy = pltpu.make_async_remote_copy(
            src_ref=src,
            dst_ref=dst,
            send_sem=self.send_sem.at[i],
            recv_sem=self.recv_sem.at[i],
            device_id=device,
            device_id_type=MESH,
        )
        copy.start()
        self.started.append(copy)
        return copy

    def local(self, src, dst):
        i = self.local_count
        self.local_count += 1
        copy = pltpu.make_async_copy(src, dst, self.local_sem.at[i])
        copy.start()
        return copy

    def finish_sends(self):
        for copy in self.started:
            copy.wait_send()


def greet(devices):
    barrier = pltpu.get_barrier_semaphore()
    for device in devices:
        pl.semaphore_signal(barrier, inc=1, device_id=device, device_id_type=MESH)
    pl.semaphore_wait(barrier, len(devices))


def place():
    s = lax.axis_index("seq")
    x, y, c = s // 8, lax.rem(s // 2, 4), lax.rem(s, 2)

    def at(dx, dy, other=0):
        core = c if other == 0 else 1 - c
        return {"seq": (lax.rem(x + dx + 4, 4) * 4 + lax.rem(y + dy + 4, 4)) * 2 + core}

    return x, y, c, at


SLOTS = ((1, 4), (1, 3), (1, 2), (2, 4), (2, 3), (3, 4))


def wrap4(i):
    return lax.rem(i + 4, 4)


def spread_kernel(
    q_ref, o_ref, g_ref, k_ref, v_ref,
    qo_ref, go_ref, dp_ref, kf_ref, vf_ref,
    o_buf, g_buf, d_buf, relay, d_relay, send_sem, recv_sem, local_sem,
):
    me = lax.axis_index("kv")
    x, y, c, at = place()
    z_at = {sign: {"kv": lax.rem(me + 8 + sign, 8)} for sign in (1, -1)}
    greet([z_at[1], z_at[-1], at(1, 0), at(-1, 0), at(0, 1), at(0, -1), at(0, 0, 1)])
    wires = Wires(send_sem, recv_sem, local_sem)
    locals_ = []
    waits = []

    load_o = wires.local(o_ref, o_buf)
    load_g = wires.local(g_ref, g_buf)

    class Ring:
        def __init__(self, src, full, x_first):
            self.src, self.full, self.x_first = src, full, x_first

        def dev(self, da, db):
            return at(da, db) if self.x_first else at(db, da)

        def slot(self, da, db, half=None):
            dx, dy = (da, db) if self.x_first else (db, da)
            ref = self.full.at[wrap4(x + dx), wrap4(y + dy), c]
            return ref if half is None else ref.at[pl.ds(half * 256, 256)]

        def put(self, ref, da, db):
            return wires.send(ref, ref, self.dev(da, db))

        def share(self, da, db):
            ref = self.slot(da, db)
            waits.append(wires.send(ref, ref, at(0, 0, 1)))

        def begin(self):
            own = self.slot(0, 0)
            self.ap = wires.send(self.src, own, self.dev(1, 0))
            self.am = wires.send(self.src, own, self.dev(-1, 0))
            self.bp = [wires.send(self.src, own, self.dev(0, 1))]
            self.bm = [wires.send(self.src, own, self.dev(0, -1))]

        def own(self):
            own = self.slot(0, 0)
            waits.append(wires.send(self.src, own, at(0, 0, 1)))
            locals_.append(wires.local(self.src, own))

        def both(self, ref):
            self.bp.append(self.put(ref, 0, 1))
            self.bm.append(self.put(ref, 0, -1))

        def first(self):
            self.ap.wait_recv()
            self.a2p = self.put(self.slot(-1, 0, 0), 1, 0)
            self.both(self.slot(-1, 0))
            self.am.wait_recv()
            self.a2m = self.put(self.slot(1, 0, 1), -1, 0)
            self.both(self.slot(1, 0))
            self.share(-1, 0)
            self.share(1, 0)

        def second(self):
            self.a2p.wait_recv()
            self.both(self.slot(2, 0, 0))
            self.a2m.wait_recv()
            self.both(self.slot(2, 0, 1))
            self.share(2, 0)

        def third(self, step):
            if step == 0:
                self.bp[0].wait_recv()
                self.c = [self.put(self.slot(0, -1), 0, 1)]
                self.share(0, -1)
                self.bm[0].wait_recv()
                self.share(0, 1)
            elif step == 1:
                self.bp[1].wait_recv()
                self.c.append(self.put(self.slot(-1, -1), 0, 1))
                self.share(-1, -1)
                self.bm[1].wait_recv()
                self.share(-1, 1)
            elif step == 2:
                self.bp[2].wait_recv()
                self.share(1, -1)
                self.bm[2].wait_recv()
                self.c.append(self.put(self.slot(1, 1), 0, -1))
                self.share(1, 1)
            else:
                self.bm[3].wait_recv()
                self.c.append(self.put(self.slot(2, 1, 0), 0, -1))
                self.bm[4].wait_recv()
                self.c.append(self.put(self.slot(2, 1, 1), 0, -1))
                self.share(2, 1)
                self.bp[3].wait_recv()
                self.bp[4].wait_recv()
                self.share(2, -1)

        def fourth(self, step):
            if step < 3:
                self.c[step].wait_recv()
                self.share((0, -1, 1)[step], 2)
            else:
                self.c[3].wait_recv()
                self.c[4].wait_recv()
                self.share(2, 2)

    rings = (Ring(k_ref.at[0], kf_ref, True), Ring(v_ref.at[0], vf_ref, False))
    for ring in rings:
        ring.begin()
    rows = pl.ds(pl.multiple_of(me * 32, 32), 32)

    def columns(i):
        return pl.ds(pl.multiple_of(lax.rem(me + i, 8) * 1024, 1024), 1024)

    moved = {}

    def z_hop(hop, far):
        for a, (src, dst) in enumerate(((q_ref, qo_ref), (g_ref, go_ref))):
            for side, sign in enumerate((1, -1)):
                first, count = (16 * side, 16) if far == 4 else (0, 32)
                if hop == 1:
                    part = src.at[pl.ds(first, count), columns(8 + sign * far)]
                else:
                    moved[a, side, hop - 1, far].wait_recv()
                    part = relay.at[a, side, SLOTS.index((hop - 1, far)), pl.ds(0, count)]
                if hop == far:
                    start = lax.rem(me + 8 - sign * (hop - 1), 8) * 32 + first
                    there = dst.at[pl.ds(pl.multiple_of(start, 16), count), :]
                else:
                    there = relay.at[a, side, SLOTS.index((hop, far)), pl.ds(0, count)]
                copy = wires.send(part, there, z_at[sign])
                moved[a, side, hop, far] = copy
                if hop == far:
                    waits.append(copy)

    def delta_hop(hop, far):
        for side, sign in enumerate((1, -1) if far < 4 else (1,)):
            if hop == 1:
                part = d_buf.at[lax.rem(me + 8 + sign * far, 8)]
            else:
                moved[2, side, hop - 1, far].wait_recv()
                part = d_relay.at[side, SLOTS.index((hop - 1, far))]
            if hop == far:
                there = dp_ref.at[lax.rem(me + 8 - sign * (hop - 1), 8)]
            else:
                there = d_relay.at[side, SLOTS.index((hop, far))]
            copy = wires.send(part, there, z_at[sign])
            moved[2, side, hop, far] = copy
            if hop == far:
                waits.append(copy)

    for far in (4, 3, 2):
        z_hop(1, far)
    for src, dst in ((q_ref, qo_ref), (g_ref, go_ref)):
        locals_.append(wires.local(src.at[:, columns(0)], dst.at[rows, :]))
    for ring in rings:
        ring.own()

    load_o.wait()
    load_g.wait()
    of_head = (
        lax.broadcasted_iota(jnp.int32, (8, 1024), 1) // 128
        == lax.broadcasted_iota(jnp.int32, (8, 1024), 0)
    ).astype(jnp.float32)
    d_buf[...] = jnp.zeros(d_buf.shape, jnp.float32)
    for group in range(8):
        cols = pl.ds(group * 1024, 1024)
        terms = o_buf[:, cols].astype(jnp.float32) * g_buf[:, cols].astype(jnp.float32)
        d_buf[group, :, :32] = lax.dot_general(
            of_head,
            terms,
            (((1,), (1,)), ((), ())),
            precision=lax.Precision.HIGHEST,
            preferred_element_type=jnp.float32,
        )
    for far in (4, 3, 2, 1):
        delta_hop(1, far)
    z_hop(1, 1)
    locals_.append(wires.local(d_buf.at[me], dp_ref.at[me]))

    for ring in rings:
        ring.first()
    for far in (4, 3, 2):
        z_hop(2, far)
        delta_hop(2, far)
    for ring in rings:
        ring.second()
    for step in range(2):
        for ring in rings:
            ring.third(step)
    for far in (4, 3):
        z_hop(3, far)
        delta_hop(3, far)
    for step in range(2, 4):
        for ring in rings:
            ring.third(step)
    z_hop(4, 4)
    delta_hop(4, 4)
    for step in (0, 2, 1, 3):
        for ring in rings:
            ring.fourth(step)
    for copy in waits:
        copy.wait_recv()
    for copy in locals_:
        copy.wait()
    wires.finish_sends()


def collect_kernel(
    dq_ref, sum_ref,
    gq_ref, gkv_ref,
    stage_k, stage_v, mine_k, mine_v, sib_k, sib_v, far_k, far_v, near_k, near_v, end_k, end_v, relay,
    send_sem, recv_sem, local_sem,
):
    me = lax.axis_index("kv")
    x, y, c, at = place()
    z_at = {sign: {"kv": lax.rem(me + 8 + sign, 8)} for sign in (1, -1)}
    greet([z_at[1], z_at[-1], at(1, 0), at(-1, 0), at(0, 1), at(0, -1), at(0, 0, 1)])
    wires = Wires(send_sem, recv_sem, local_sem)
    f32, bf16 = jnp.float32, jnp.bfloat16
    waits = []
    lo, hi = pl.ds(0, 256), pl.ds(256, 256)
    order = (
        (2, 2), (-1, 2), (1, 2), (0, 2),
        (-1, 1), (2, -1), (1, -1),
        (2, 1), (-1, -1), (1, 1), (0, -1), (0, 1),
        (2, 0), (1, 0), (-1, 0), (0, 0),
    )

    class Ring:
        def __init__(self, first, stage, mine, sib, far, near, end, x_first):
            self.first, self.stage, self.mine, self.sib = first, stage, mine, sib
            self.far, self.near, self.end, self.x_first = far, near, end, x_first
            self.swaps, self.fars, self.nears = {}, {}, {}

        def dev(self, da, db):
            return at(da, db) if self.x_first else at(db, da)

        def cell(self, ref, da, db):
            dx, dy = (da, db) if self.x_first else (db, da)
            return ref.at[wrap4(x + dx), wrap4(y + dy)]

        def sums(self, da, db, core):
            dx, dy = (da, db) if self.x_first else (db, da)
            owner = (wrap4(x + dx) * 4 + wrap4(y + dy)) * 2 + core
            cols = pl.ds(self.first, 128)
            return sum_ref[pl.ds(owner * 4, 4), :, cols].reshape(512, 128)

        def swap(self, da, db):
            there = self.cell(self.stage, da, db)
            there[...] = self.sums(da, db, 1 - c).astype(bf16)
            self.swaps[da, db] = wires.send(there, self.cell(self.sib, da, db), at(0, 0, 1))

        def pair(self, da, db):
            self.swaps[da, db].wait_recv()
            return self.sums(da, db, c) + self.cell(self.sib, da, db)[...].astype(f32)

        def send(self, piece, da, db, dst, device):
            m = self.cell(self.mine, da, db)
            m[...] = piece.astype(bf16)
            return wires.send(m, dst, device)

        def to_far(self, da):
            up = da > 0
            side = 0 if up else 1
            i = (2, 1).index(da) if up else (-1, 0).index(da)
            self.fars[da] = self.send(
                self.pair(da, 2), da, 2, self.far.at[side, i], self.dev(0, 1 if up else -1)
            )

        def to_near(self, da, db):
            piece = self.pair(da, db)
            side = 0 if db == 1 else 1
            if (da > 0) == (db == 1):
                i = (2, 1).index(da) if da > 0 else (-1, 0).index(da)
                self.fars[da].wait_recv()
                piece = piece + self.far[side, i].astype(f32)
            self.nears[da, db] = self.send(
                piece, da, db, self.near.at[side, da % 4], self.dev(0, db)
            )

        def total(self, da):
            piece = self.pair(da, 0)
            self.nears[da, -1].wait_recv()
            piece = piece + self.near[1, da % 4].astype(f32)
            self.nears[da, 1].wait_recv()
            return piece + self.near[0, da % 4].astype(f32)

        def turn(self):
            m = self.cell(self.mine, 2, 0)
            m[...] = self.total(2).astype(bf16)
            self.end_far_p = wires.send(m.at[lo], self.end.at[0, lo], self.dev(1, 0))
            self.end_far_m = wires.send(m.at[hi], self.end.at[0, hi], self.dev(-1, 0))

        def side(self, da):
            m = self.cell(self.mine, da, 0)
            piece = self.total(da)
            if da == 1:
                m[hi] = piece[256:].astype(bf16)
                self.end_far_p.wait_recv()
                m[lo] = (piece[:256] + self.end[0, lo].astype(f32)).astype(bf16)
                self.end_p = wires.send(m, self.end.at[1], self.dev(1, 0))
            else:
                m[lo] = piece[:256].astype(bf16)
                self.end_far_m.wait_recv()
                m[hi] = (piece[256:] + self.end[0, hi].astype(f32)).astype(bf16)
                self.end_m = wires.send(m, self.end.at[2], self.dev(-1, 0))

        def last(self, out, scale):
            t = self.total(0)
            self.end_p.wait_recv()
            t = t + self.end[1].astype(f32)
            self.end_m.wait_recv()
            t = t + self.end[2].astype(f32)
            out[...] = (t * scale).astype(bf16)

    rings = (
        Ring(0, stage_k, mine_k, sib_k, far_k, near_k, end_k, True),
        Ring(128, stage_v, mine_v, sib_v, far_v, near_v, end_v, False),
    )
    def columns(i):
        return pl.ds(pl.multiple_of(lax.rem(me + 8 + i, 8) * 1024, 1024), 1024)

    moved = {}

    def z_hop(hop, far):
        for side, sign in enumerate((1, -1)):
            first, count = (16 * side, 16) if far == 4 else (0, 32)
            if hop == 1:
                start = lax.rem(me + 8 + sign * far, 8) * 32 + first
                part = dq_ref.at[pl.ds(pl.multiple_of(start, 16), count), :]
            else:
                moved[side, hop - 1, far].wait_recv()
                part = relay.at[side, SLOTS.index((hop - 1, far)), pl.ds(0, count)]
            if hop == far:
                there = gq_ref.at[pl.ds(first, count), columns(-sign * (hop - 1))]
            else:
                there = relay.at[side, SLOTS.index((hop, far)), pl.ds(0, count)]
            copy = wires.send(part, there, z_at[sign])
            moved[side, hop, far] = copy
            if hop == far:
                waits.append(copy)

    def swaps(part):
        for da, db in part:
            for ring in rings:
                ring.swap(da, db)

    swaps(order[:2])
    for step, (da, db) in enumerate(order[:12]):
        for ring in rings:
            if db == 2:
                ring.to_far(da)
            else:
                ring.to_near(da, db)
        if step == 0:
            swaps(order[2:5])
        elif step == 1:
            swaps(order[5:9])
        elif step == 2:
            swaps(order[9:])
        elif step == 3:
            for far in (4, 3, 2, 1):
                z_hop(1, far)
        elif step == 7:
            for far in (4, 3, 2):
                z_hop(2, far)
    mine = pl.ds(pl.multiple_of(me * 32, 32), 32)
    own = wires.local(dq_ref.at[mine, :], gq_ref.at[:, columns(0)])
    for far in (4, 3):
        z_hop(3, far)
    for ring in rings:
        ring.turn()
    z_hop(4, 4)
    for da in (1, -1):
        for ring in rings:
            ring.side(da)
    rings[0].last(gkv_ref.at[0], 1.0 / math.sqrt(128.0))
    rings[1].last(gkv_ref.at[1], 1.0)
    for copy in waits:
        copy.wait_recv()
    own.wait()
    wires.finish_sends()


ANY = pl.BlockSpec(memory_space=pl.ANY)
HBM = pl.BlockSpec(memory_space=pltpu.HBM)
VM = pl.BlockSpec(memory_space=pltpu.VMEM)
SM = pl.BlockSpec(memory_space=pltpu.SMEM)
DMA = pltpu.SemaphoreType.DMA


def spread(q, o, g, k, v):
    bf16 = jnp.bfloat16
    rows = jax.ShapeDtypeStruct((256, 1024), bf16)
    cache = jax.ShapeDtypeStruct((4, 4, 2, 512, 128), bf16)
    return pl.pallas_call(
        spread_kernel,
        out_shape=(rows, rows, jax.ShapeDtypeStruct((8, 8, 128), jnp.float32), cache, cache),
        in_specs=[HBM] * 5,
        out_specs=(ANY,) * 5,
        scratch_shapes=[
            pltpu.VMEM((32, 8192), bf16),
            pltpu.VMEM((32, 8192), bf16),
            pltpu.VMEM((8, 8, 128), jnp.float32),
            pltpu.VMEM((2, 2, 6, 32, 1024), bf16),
            pltpu.VMEM((2, 6, 8, 128), jnp.float32),
            DMA((144,)),
            DMA((144,)),
            DMA((8,)),
        ],
        compiler_params=pltpu.CompilerParams(
            collective_id=0, has_side_effects=True, vmem_limit_bytes=4 * 2**20
        ),
    )(q, o, g, k, v)


def collect(dq, sums):
    bf16 = jnp.bfloat16
    out = jax.ShapeDtypeStruct((2, 512, 128), bf16)
    return pl.pallas_call(
        collect_kernel,
        out_shape=(jax.ShapeDtypeStruct((32, 8192), bf16), out),
        in_specs=[ANY, VM],
        out_specs=(ANY, VM),
        scratch_shapes=[
            pltpu.VMEM((4, 4, 512, 128), bf16),
            pltpu.VMEM((4, 4, 512, 128), bf16),
            pltpu.VMEM((4, 4, 512, 128), bf16),
            pltpu.VMEM((4, 4, 512, 128), bf16),
            pltpu.VMEM((4, 4, 512, 128), bf16),
            pltpu.VMEM((4, 4, 512, 128), bf16),
            pltpu.VMEM((2, 2, 512, 128), bf16),
            pltpu.VMEM((2, 2, 512, 128), bf16),
            pltpu.VMEM((2, 4, 512, 128), bf16),
            pltpu.VMEM((2, 4, 512, 128), bf16),
            pltpu.VMEM((3, 512, 128), bf16),
            pltpu.VMEM((3, 512, 128), bf16),
            pltpu.VMEM((2, 6, 32, 1024), bf16),
            DMA((96,)),
            DMA((96,)),
            DMA((1,)),
        ],
        compiler_params=pltpu.CompilerParams(
            collective_id=1, has_side_effects=True, vmem_limit_bytes=22 * 2**20
        ),
    )(dq, sums)


def on_device(
    query_rows, attn_out, grad_out, logsumexp, key_cache, value_cache, block_lists, block_counts
):
    def stay(a):
        return pltpu.with_memory_space_constraint(a, pltpu.HBM)

    q, g, dp, kf, vf = spread(
        stay(query_rows), stay(attn_out), stay(grad_out), stay(key_cache), stay(value_cache)
    )
    blocks = (128, 128, 128)
    dq, sums = grads(
        stay(block_lists),
        stay(block_counts.T),
        q,
        g,
        stay(logsumexp),
        dp,
        kf.reshape(blocks),
        vf.reshape(blocks),
    )
    gq, pair = collect(dq, sums)
    return gq, pair[:1], pair[1:]


def solution(mesh):
    placed = (
        P(("seq", "kv"), None),
        P(("seq", "kv"), None),
        P(("seq", "kv"), None),
        P("kv", "seq"),
        P("kv", "seq", None),
        P("kv", "seq", None),
        P("kv", "seq", None),
        P("kv", "seq"),
    )
    return jax.shard_map(
        on_device,
        mesh=mesh,
        in_specs=placed,
        out_specs=(P(("seq", "kv"), None), P("kv", "seq", None), P("kv", "seq", None)),
        check_vma=False,
    )
```
